512 devices in a mesh: gx: 16 (over z), gy: 8 (over x, core), gz: 4 (over y).
Axes of the slice: x: 4, y: 4, z: 16, core: 2. Of those that a mesh axis runs over, the one named last changes fastest.
Arguments:
- state: float32 [4, 128, 64, 512], P(None, 'gx', 'gy', 'gz'), may hold values from -6 to 6
- sample_cell: int32 [524288], P(('gx', 'gy', 'gz')), may hold values from 0 to 8191
- sample_dest: int32 [524288, 1], P(('gx', 'gy', 'gz')), may hold values from 0 to 63; in each aligned block of 1024 rows (0 to 1023, 1024 to 2047, ...) at most 32 rows name the same one
- sample_weight: float32 [524288], P(('gx', 'gy', 'gz')), may hold values from 0.05 to 0.5
- sample_elem: int32 [524288], P(('gx', 'gy', 'gz')), may hold values from 0 to 127
- element_motion: float32 [3, 8192], P(None, ('gx', 'gz')), may hold values from -6 to 6
- element_coef: float32 [8192], P(('gx', 'gz')), may hold values from 0.01 to 0.1
Outputs:
- new_state: float32 [4, 128, 64, 512], P(None, 'gx', 'gy', 'gz')
- body_force: float32 [3, 128, 64, 512], P(None, 'gx', 'gy', 'gz')
The draws below stay inside these ranges and needn't reach their ends.
Inputs may be any that keep to these rules, and one draw needn't show every extreme that they name: `sample_dest`: in the 1024 rows of one device no turbine-section device is named more than 32 times; some device names one exactly 32 times.
All inputs are finite; a program needn't handle non-finite values.
Results may differ from the reference program's by a relative error of at most 0.00012.
Values sent between devices are 32-bit elements; how exact they have to be, the bound alone decides.
No kernel may reach another device: no remote copies, remote signals or barrier semaphores. Data moves between devices by JAX's collectives and lax.ppermute only.
A program may use at most 64 MiB of HBM per device.

```python
import math
import jax
import jax.numpy as jnp
import numpy as np
from jax import lax

CX = 8
CY = 8
CZ = 128
SAMP_DEV = 1024
ELEM_DEV = 128
CAP = 32
CELLS = 8192
NX = 128
NY = 64
NZ = 512
SAMPLES = 524288
ELEMENTS = 8192
N_GX = 16
N_GY = 8
N_GZ = 4


def set_ends(array, stream_key, smallest, largest):
    longest = array.shape.index(max(array.shape))
    spots = []
    for shift in (0, 1):
        where = [jax.random.randint(jax.random.fold_in(stream_key, axis), (), 0, length) for axis, length in enumerate(array.shape)]
        where[longest] = (where[longest] + shift) % array.shape[longest]
        spots.append(tuple(where))
    return array.at[spots[0]].set(smallest).at[spots[1]].set(largest)


def level_of(key, dims, split, least, high):
    gain = 1.0
    for dim, blocks in split:
        heights = jax.random.uniform(jax.random.fold_in(jax.random.fold_in(key, 6), dim), (blocks,), jnp.float32, least / len(split), high / len(split))
        gain = gain * jnp.repeat(jnp.exp(heights), dims[dim] // blocks).reshape((-1,) + (1,) * (len(dims) - 1 - dim))
    return gain


def shared_out(stream_key, own, number, rows, count, top, most, skew):
    sequence = jax.random.permutation(stream_key, count)
    heavy_load, common = shares(count, rows * top, most, skew, True), shares(count, rows * top, most, skew, False)
    places = jnp.arange(count)

    def named(tallies, offset_by):
        used = int((tallies > 0).sum())
        fixed = max(1, used // 4)
        passed = fixed + (places - fixed + offset_by * (used - fixed)) % max(1, count - fixed)
        return jnp.zeros((count,), jnp.int32).at[sequence[jnp.where(places < fixed, places, passed)]].set(jnp.asarray(tallies, jnp.int32))

    tallies = jnp.where(number % 4 == 0, named(heavy_load, number // 4), named(common, number - number // 4 - 1))
    mixed = jax.random.permutation(jax.random.fold_in(own, 3), count)
    donor, receiver = mixed[0:count // 2 * 2:2], mixed[1:count // 2 * 2:2]
    slack = jnp.minimum(tallies[donor] - 1, most - tallies[receiver]) // 2
    slack = jnp.where((donor == sequence[0]) | (receiver == sequence[0]) | (tallies[receiver] == 0), 0, jnp.maximum(slack, 0))
    passed = jax.random.randint(jax.random.fold_in(own, 4), (count // 2,), 0, 1 << 20) % (slack + 1)
    tallies = tallies.at[donor].add(-passed).at[receiver].add(passed)
    labels = jnp.searchsorted(jnp.cumsum(tallies), jnp.arange(rows * top), side="right").astype(jnp.int32)
    table = labels.reshape(top, rows).T
    table = table[jax.random.permutation(jax.random.fold_in(own, 1), rows)]
    offset_by = jax.random.randint(jax.random.fold_in(own, 2), (rows, 1), 0, top)
    return jnp.take_along_axis(table, (jnp.arange(top)[None, :] + offset_by) % top, axis=1)


def shares(number_of, total, bound, slope, full):
    weights = [(1 << 20) // math.isqrt(grade ** slope) + 1 for grade in range(1, number_of + 1)]
    largest = bound if full else min(bound, max(-(-total // number_of), total * weights[0] // sum(weights)))
    least = 1 if total - largest >= number_of - 1 else 0
    given, rest = [largest] + [least] * (number_of - 1), total - largest - least * (number_of - 1)
    while rest > 0:
        candidates = [i for i in range(1, number_of) if given[i] < largest] or [i for i in range(1, number_of) if given[i] < bound]
        whole, remaining = sum([weights[i] for i in candidates]), rest
        for i in candidates:
            addition = min(bound - given[i], max(1, remaining * weights[i] // whole), rest)
            given[i] = given[i] + addition
            rest = rest - addition
    return np.array(given)


def scatter_about(stream_key, shape, scale, limit, pieces=(), held_as=jnp.bfloat16):
    drawn = scale * jax.random.normal(stream_key, shape, jnp.float32)
    if pieces:
        drawn = drawn * level_of(stream_key, shape, pieces, -0.22, 0.18)
    return jnp.clip(drawn, -limit, limit).astype(held_as)


def setup_inputs(seed: int = 0) -> dict:
    arg_keys = jax.random.split(jax.random.key(seed), 8)
    state = scatter_about(arg_keys[0], (4, NX, NY, NZ), 1.0, 6.0, ((1, 16), (2, 8), (3, 4)), jnp.float32)
    sample_cell = set_ends(jax.random.randint(arg_keys[1], (SAMPLES,), 0, CELLS), jax.random.fold_in(arg_keys[1], 1), 0, CELLS - 1).astype(jnp.int32)
    sample_dest_keys = jax.random.split(jax.random.fold_in(arg_keys[2], 1), SAMPLES // SAMP_DEV)
    sample_dest_turns = jax.random.permutation(jax.random.fold_in(arg_keys[2], 3), SAMPLES // SAMP_DEV)
    sample_dest = jax.vmap(lambda own, number: shared_out(jax.random.fold_in(arg_keys[2], 2), own, number, SAMP_DEV, N_GX * N_GZ, 1, CAP, 2))(sample_dest_keys, sample_dest_turns).reshape((SAMPLES, 1))
    sample_weight = jnp.clip(jnp.exp(math.log(0.5) - 2.3025851 * jax.random.uniform(arg_keys[3], (SAMPLES,), jnp.float32) ** level_of(arg_keys[3], (SAMPLES,), ((0, 512),), -0.2, 0.2)), 0.05, 0.5)
    sample_elem = set_ends(jax.random.randint(arg_keys[4], (SAMPLES,), 0, ELEM_DEV), jax.random.fold_in(arg_keys[4], 1), 0, ELEM_DEV - 1).astype(jnp.int32)
    element_motion = scatter_about(arg_keys[5], (3, ELEMENTS), 1.0, 6.0, ((1, 64),), jnp.float32)
    element_coef = jnp.clip(jnp.exp(math.log(0.1) - 2.3025851 * jax.random.uniform(arg_keys[6], (ELEMENTS,), jnp.float32) ** level_of(arg_keys[6], (ELEMENTS,), ((0, 64),), -0.2, 0.2)), 0.01, 0.1)
    return dict(state=state, sample_cell=sample_cell, sample_dest=sample_dest, sample_weight=sample_weight, sample_elem=sample_elem, element_motion=element_motion, element_coef=element_coef)


DT_STEP = 0.4
BASE_COEF = 0.02
PRANDTL = 0.7
SMAG_COEF = 0.04

def shifted(padded, axis, offset):
    lead = padded.ndim - 3
    parts = [slice(None)] * lead + [slice(1, -1)] * 3
    length = padded.shape[lead + axis]
    parts[lead + axis] = slice(1 + offset, length - 1 + offset)
    return padded[tuple(parts)]

def eddy(padded):
    grads = [[0.5 * (shifted(padded[c], j, 1) - shifted(padded[c], j, -1)) for j in range(3)] for c in range(3)]
    strain = 0.0
    for c in range(3):
        for j in range(3):
            paired = 0.5 * (grads[c][j] + grads[j][c])
            strain = strain + paired * paired
    return SMAG_COEF * jnp.sqrt(2.0 * strain)

def advance(padded, viscous, force):
    centre_visc = shifted(viscous, 0, 0)
    result = []
    for c in range(4):
        values = padded[c]
        middle = shifted(values, 0, 0)
        ratio = 1.0 if c < 3 else 1.0 / PRANDTL
        change = jnp.zeros_like(middle)
        for j in range(3):
            upper = shifted(values, j, 1)
            lower = shifted(values, j, -1)
            upper_coef = BASE_COEF + ratio * 0.5 * (centre_visc + shifted(viscous, j, 1))
            lower_coef = BASE_COEF + ratio * 0.5 * (centre_visc + shifted(viscous, j, -1))
            change = change + upper_coef * (upper - middle) - lower_coef * (middle - lower)
            change = change - shifted(padded[j], 0, 0) * 0.5 * (upper - lower)
        if c < 3:
            change = change + force[c]
        result.append(middle + DT_STEP * change)
    return jnp.stack(result)

def pad_grid(values, width):
    lead = values.ndim - 3
    wrapped = jnp.pad(values, [(0, 0)] * lead + [(width, width), (width, width), (0, 0)], mode='wrap')
    return jnp.pad(wrapped, [(0, 0)] * lead + [(0, 0), (0, 0), (width, width)])

def reference(state, sample_cell, sample_dest, sample_weight, sample_elem, element_motion, element_coef):
    total_rows = sample_cell.shape[0]
    rows = jnp.arange(total_rows, dtype=jnp.int32)
    device = rows // SAMP_DEV
    plane_x = device // (N_GY * N_GZ)
    plane_y = device // N_GZ % N_GY
    plane_z = device % N_GZ
    local_x = sample_cell // (CY * CZ)
    local_y = sample_cell // CZ % CY
    local_z = sample_cell % CZ
    global_cell = ((plane_x * CX + local_x) * NY + plane_y * CY + local_y) * NZ + plane_z * CZ + local_z
    velocity = state[:3].reshape(3, -1)
    sampled = velocity[:, global_cell] * sample_weight
    element = sample_dest[:, 0] * ELEM_DEV + sample_elem
    point_velocity = jax.ops.segment_sum(sampled.T, element, num_segments=ELEMENTS).T
    relative = point_velocity + element_motion
    speed = jnp.sqrt(lax.optimization_barrier(jnp.sum(relative * relative, axis=0)))
    element_force = -element_coef * speed * relative
    spread = element_force[:, element] * sample_weight
    body_force = jax.ops.segment_sum(spread.T, global_cell, num_segments=NX * NY * NZ).T.reshape(3, NX, NY, NZ)
    padded = pad_grid(state, 1)
    viscous = pad_grid(eddy(padded), 1)
    new_state = advance(padded, viscous, body_force)
    return (new_state, body_force)
```

```python
import jax
import jax.numpy as jnp
from jax import lax
from jax.experimental import pallas as pl
from jax.experimental.pallas import tpu as pltpu
from jax.sharding import PartitionSpec as P

DT_STEP = 0.4
BASE_COEF = 0.02
PRANDTL = 0.7
SMAG_COEF = 0.04

ROWS = 1024
PLANE = ("gy", "gz")


def call(kernel, outs, scratch=(), smem=0, count=1, flops=2_000_000, nbytes=1_000_000):
    return pl.pallas_call(
        kernel,
        out_shape=outs,
        in_specs=[pl.BlockSpec(memory_space=pltpu.SMEM)] * smem
        + [pl.BlockSpec(memory_space=pltpu.VMEM)] * (count - smem),
        out_specs=jax.tree.map(lambda _: pl.BlockSpec(memory_space=pltpu.VMEM), outs),
        scratch_shapes=scratch,
        compiler_params=pltpu.CompilerParams(vmem_limit_bytes=24 * 1024 * 1024),
        cost_estimate=pl.CostEstimate(flops=flops, bytes_accessed=nbytes, transcendentals=0),
    )


def f32(*shape):
    return jax.ShapeDtypeStruct(shape, jnp.float32)


def halves(values):
    high = values.astype(jnp.bfloat16)
    return high, (values - high.astype(jnp.float32)).astype(jnp.bfloat16)


def onehot(index, size):
    wanted = lax.broadcasted_iota(jnp.int32, (size, ROWS), 0)
    return jnp.where(wanted == index, 1.0, 0.0).astype(jnp.bfloat16)


def pick(table, hot):
    both = jnp.concatenate(halves(table), axis=1)
    return jnp.dot(both, jnp.concatenate([hot, hot], axis=0), preferred_element_type=jnp.float32)


def put(values, hot):
    high, low = halves(values)
    dims = (((1,), (1,)), ((), ()))
    total = lax.dot_general(high, hot, dims, preferred_element_type=jnp.float32)
    return total + lax.dot_general(low, hot, dims, preferred_element_type=jnp.float32)


def cell_keys(cell):
    column = lax.broadcasted_iota(jnp.int32, (64, ROWS), 0) == (cell >> 7)
    return column, onehot(cell & 127, 128)


def element_keys(dest, elem):
    tile = (elem >> 4) * 4 + (dest & 3)
    along = dest >> 2
    number = tile * 2 + (along >> 3)
    shape = (32, 8, ROWS)
    row = lax.broadcasted_iota(jnp.int32, shape, 0) * 2 + (
        lax.broadcasted_iota(jnp.int32, shape, 1) & 1
    )
    return row == number[None], onehot((along & 7) * 16 + (elem & 15), 128)


def sample_kernel(state, cell, dest, elem, weight, out):
    column, hot_z = cell_keys(cell[...])
    found = pick(state[0:3].reshape(192, 128), hot_z).reshape(3, 64, ROWS)
    sampled = [
        jnp.sum(jnp.where(column, found[c], 0.0), axis=0, keepdims=True) * weight[...]
        for c in range(3)
    ]
    row = lax.broadcasted_iota(jnp.int32, (8, ROWS), 0) >> 1
    pattern = jnp.where(
        row == 0, sampled[0], jnp.where(row == 1, sampled[1], jnp.where(row == 2, sampled[2], 0.0))
    )
    match, hot_lane = element_keys(dest[...], elem[...])
    spread = jnp.where(match, pattern[None], 0.0).reshape(256, ROWS)
    out[...] = put(spread, hot_lane).reshape(32, 8, 128)


def own_kernel(place, parts, motion, coef, out):
    gx, gy = place[0], place[1]
    total = jnp.sum(parts[...], axis=0)
    row = lax.broadcasted_iota(jnp.int32, (8, 128), 0)
    lane = lax.broadcasted_iota(jnp.int32, (8, 128), 1)
    level = row >> 1
    held = jnp.where(
        level == 0,
        motion[0:1, :],
        jnp.where(level == 1, motion[1:2, :], jnp.where(level == 2, motion[2:3, :], coef[...])),
    )
    moved = pltpu.roll(held, ((gx & 7) * 16 - gy * 16 + 128) & 127, 1)
    mine = ((lane >> 4) == (gx & 7)) & ((row & 1) == (gx >> 3))
    total = total + jnp.where(mine, moved, 0.0)
    out[...] = jnp.broadcast_to(total[None], (16, 8, 128))


def force_kernel(parts, out):
    total = jnp.sum(parts[...], axis=0)
    row = lax.broadcasted_iota(jnp.int32, (8, 128), 0)

    def by_parity(values):
        values = values + pltpu.roll(values, 4, 0)
        return values + pltpu.roll(values, 2, 0)

    speed = jnp.sqrt(by_parity(jnp.where(row < 6, total * total, 0.0)))
    coef = by_parity(jnp.where(row < 6, 0.0, total))
    force = jnp.where(row < 6, -coef * speed * total, 0.0)
    out[...] = jnp.broadcast_to(force[None], (32, 8, 128))


def spread_kernel(forces, cell, dest, elem, weight, before, new_state, body_force):
    match, hot_lane = element_keys(dest[...], elem[...])
    found = pick(forces[...].reshape(256, 128), hot_lane).reshape(32, 8, ROWS)
    pairs = jnp.sum(jnp.where(match, found, 0.0), axis=0)
    column, hot_z = cell_keys(cell[...])
    each = [(pairs[2 * c : 2 * c + 1] + pairs[2 * c + 1 : 2 * c + 2]) * weight[...] for c in range(3)]
    spread = jnp.concatenate([jnp.where(column, each[c], 0.0) for c in range(3)], axis=0)
    body = put(spread, hot_z).reshape(3, 8, 8, 128)
    body_force[...] = body
    new_state[0:3] = before[0:3] + DT_STEP * body
    new_state[3] = before[3]


def fill(grid, state, xlo, xhi, ylo, yhi):
    grid[:, 2:10, 0:8, 0:128] = state[...]
    grid[:, 0:2, 0:8, 0:128] = xlo[...]
    grid[:, 10:12, 0:8, 0:128] = xhi[...]
    grid[:, 1:11, 8:10, 0:128] = yhi[...]
    grid[:, 1:11, 14:16, 0:128] = ylo[...]


def ends_kernel(state, xlo, xhi, ylo, yhi, zup, zdown, grid):
    grid[:, :, 8:16, 0:128] = jnp.zeros((4, 12, 8, 128), jnp.float32)
    fill(grid, state, xlo, xhi, ylo, yhi)
    rows = grid[:, 1:11, :, 0:128].reshape(640, 128)
    row = lax.broadcasted_iota(jnp.int32, (8, 128), 0)
    lane = lax.broadcasted_iota(jnp.int32, (8, 128), 1)
    wanted = jnp.where(row < 2, row, jnp.where(row < 4, row + 124, -1))
    ends = lax.dot_general(
        jnp.where(lane == wanted, 1.0, 0.0),
        rows,
        (((1,), (1,)), ((), ())),
        precision=lax.Precision.HIGHEST,
        preferred_element_type=jnp.float32,
    )
    zdown[...] = ends[0:2]
    zup[...] = ends[2:4]


def stencil_kernel(place, state, xlo, xhi, ylo, yhi, zlo, zhi, out, grid):
    gz = place[2]
    fill(grid, state, xlo, xhi, ylo, yhi)
    row = lax.broadcasted_iota(jnp.int32, (4, 128), 0)
    lane = lax.broadcasted_iota(jnp.int32, (4, 128), 1)
    wanted = jnp.where(row < 2, row, row + 124)
    ghosts = lax.dot_general(
        jnp.concatenate([zhi[...], zlo[...]], axis=0),
        jnp.where(lane == wanted, 1.0, 0.0),
        (((0,), (0,)), ((), ())),
        precision=lax.Precision.HIGHEST,
        preferred_element_type=jnp.float32,
    ).reshape(4, 10, 16, 128)
    level = lax.broadcasted_iota(jnp.int32, (1, 1, 256), 2)
    outside = ((level >= 128) & (level < 192) & (gz == 3)) | ((level >= 192) & (gz == 0))
    grid[:, 1:11, :, 128:256] = jnp.where(outside[None, :, :, 128:256], 0.0, ghosts)

    def around(values):
        return (
            (pltpu.roll(values, 15, 1), pltpu.roll(values, 1, 1)),
            (pltpu.roll(values, 255, 2), pltpu.roll(values, 1, 2)),
        )

    fields = [grid[c] for c in range(4)]
    sides = []
    diffs = []
    for c in range(4):
        middle = fields[c][1:11]
        near = ((fields[c][2:12], fields[c][0:10]),) + around(middle)
        sides.append(near)
        diffs.append([upper - lower for upper, lower in near])
    strain = 0.5 * (
        diffs[0][0] * diffs[0][0] + diffs[1][1] * diffs[1][1] + diffs[2][2] * diffs[2][2]
    )
    for i, j in ((0, 1), (0, 2), (1, 2)):
        paired = diffs[i][j] + diffs[j][i]
        strain = strain + 0.25 * paired * paired
    eddy = jnp.where(outside, 0.0, SMAG_COEF * jnp.sqrt(strain))

    def inner(values):
        return values[:, 0:8, 0:128]

    centre = inner(eddy[1:9])
    near = ((eddy[2:10], eddy[0:8]),) + around(eddy[1:9])
    faces = [[0.5 * (centre + inner(side)) for side in pair] for pair in near]
    wind = [0.5 * inner(fields[c][2:10]) for c in range(3)]
    for c in range(4):
        middle = inner(fields[c][2:10])
        ratio = 1.0 if c < 3 else 1.0 / PRANDTL
        change = 0.0
        for j in range(3):
            upper, lower = [inner(side[1:9]) for side in sides[c][j]]
            change = change + (BASE_COEF + ratio * faces[j][0]) * (upper - middle)
            change = change - (BASE_COEF + ratio * faces[j][1]) * (middle - lower)
            change = change - wind[j] * (upper - lower)
        out[c] = middle + DT_STEP * change


def swap(up, down, axis):
    count = lax.axis_size(axis)
    forward = [(i, (i + 1) % count) for i in range(count)]
    backward = [(target, source) for source, target in forward]
    return lax.ppermute(up, axis, forward), lax.ppermute(down, axis, backward)


def exchange(blocks, axes):
    return lax.all_to_all(blocks, axes, split_axis=0, concat_axis=0, tiled=True)


def body(state, sample_cell, sample_dest, sample_weight, sample_elem, element_motion, element_coef):
    place = jnp.stack([lax.axis_index(axis) for axis in ("gx", "gy", "gz")]).astype(jnp.int32)
    cell = sample_cell.reshape(1, ROWS)
    dest = sample_dest.reshape(1, ROWS)
    elem = sample_elem.reshape(1, ROWS)
    weight = sample_weight.reshape(1, ROWS)

    xlo, xhi = swap(state[:, 6:8], state[:, 0:2], "gx")
    partial = call(sample_kernel, f32(32, 8, 128), count=5)(state, cell, dest, elem, weight)
    partial = exchange(partial, PLANE)

    wide = jnp.concatenate([xlo[:, 1:2], state, xhi[:, 0:1]], axis=1)
    ylo, yhi = swap(wide[:, :, 6:8], wide[:, :, 0:2], "gy")

    totals = call(own_kernel, f32(16, 8, 128), smem=1, count=4)(
        place, partial, element_motion, element_coef.reshape(1, 128)
    )
    totals = exchange(totals, "gx")

    padded = pltpu.VMEM((4, 12, 16, 256), jnp.float32)
    zup, zdown = call(ends_kernel, (f32(2, 640), f32(2, 640)), (padded,), count=5)(
        state, xlo, xhi, ylo, yhi
    )
    zlo, zhi = swap(zup, zdown, "gz")

    forces = call(force_kernel, f32(32, 8, 128), count=1)(totals)
    forces = exchange(forces, PLANE)

    before = call(stencil_kernel, f32(4, 8, 8, 128), (padded,), smem=1, count=8)(
        place, state, xlo, xhi, ylo, yhi, zlo, zhi
    )
    return call(spread_kernel, (f32(4, 8, 8, 128), f32(3, 8, 8, 128)), count=6)(
        forces, cell, dest, elem, weight, before
    )


def solution(mesh):
    return jax.shard_map(
        body,
        mesh=mesh,
        in_specs=(
            P(None, "gx", "gy", "gz"),
            P(("gx", "gy", "gz")),
            P(("gx", "gy", "gz"), None),
            P(("gx", "gy", "gz")),
            P(("gx", "gy", "gz")),
            P(None, ("gx", "gz")),
            P(("gx", "gz")),
        ),
        out_specs=(P(None, "gx", "gy", "gz"), P(None, "gx", "gy", "gz")),
        check_vma=False,
    )
```

```python
import jax
import jax.numpy as jnp
from jax import lax
from jax.experimental import pallas as pl
from jax.experimental.pallas import tpu as pltpu
from jax.sharding import PartitionSpec as P

DT_STEP = 0.4
BASE_COEF = 0.02
PRANDTL = 0.7
SMAG_COEF = 0.04

ROWS = 1024
PLANE = ("gy", "gz")


def call(kernel, outs, scratch=(), smem=0, count=1, space=pltpu.VMEM, flops=2_000_000, nbytes=1_000_000):
    return pl.pallas_call(
        kernel,
        out_shape=outs,
        in_specs=[pl.BlockSpec(memory_space=pltpu.SMEM)] * smem
        + [pl.BlockSpec(memory_space=space)] * (count - smem),
        out_specs=jax.tree.map(lambda _: pl.BlockSpec(memory_space=pltpu.VMEM), outs),
        scratch_shapes=scratch,
        compiler_params=pltpu.CompilerParams(vmem_limit_bytes=24 * 1024 * 1024),
        cost_estimate=pl.CostEstimate(flops=flops, bytes_accessed=nbytes, transcendentals=0),
    )


def f32(*shape):
    return jax.ShapeDtypeStruct(shape, jnp.float32)


def halves(values):
    high = values.astype(jnp.bfloat16)
    return high, (values - high.astype(jnp.float32)).astype(jnp.bfloat16)


def onehot(index, size):
    wanted = lax.broadcasted_iota(jnp.int32, (size, ROWS), 0)
    return jnp.where(wanted == index, 1.0, 0.0).astype(jnp.bfloat16)


def pick(table, hot):
    both = jnp.concatenate(halves(table), axis=1)
    return jnp.dot(both, jnp.concatenate([hot, hot], axis=0), preferred_element_type=jnp.float32)


def put(values, hot):
    high, low = halves(values)
    dims = (((1,), (1,)), ((), ()))
    total = lax.dot_general(high, hot, dims, preferred_element_type=jnp.float32)
    return total + lax.dot_general(low, hot, dims, preferred_element_type=jnp.float32)


def cell_keys(cell):
    column = lax.broadcasted_iota(jnp.int32, (64, ROWS), 0) == (cell >> 7)
    return column, onehot(cell & 127, 128)


def element_keys(dest, elem):
    tile = (elem >> 4) * 4 + (dest & 3)
    along = dest >> 2
    number = tile * 2 + (along >> 3)
    shape = (32, 8, ROWS)
    row = lax.broadcasted_iota(jnp.int32, shape, 0) * 2 + (
        lax.broadcasted_iota(jnp.int32, shape, 1) & 1
    )
    return row == number[None], onehot((along & 7) * 16 + (elem & 15), 128)


def sample_kernel(state_in, cell_in, dest_in, elem_in, weight_in, out, *scratch):
    held, sems = scratch[:5], scratch[5]
    sources = (state_in.at[0:3], cell_in, dest_in, elem_in, weight_in)
    copies = [
        pltpu.make_async_copy(source, target, sems.at[i])
        for i, (source, target) in enumerate(zip(sources, held))
    ]
    for copy in copies:
        copy.start()
    for copy in copies:
        copy.wait()
    state, cell, dest, elem, weight = held
    column, hot_z = cell_keys(cell[...])
    found = pick(state[...].reshape(192, 128), hot_z).reshape(3, 64, ROWS)
    sampled = [
        jnp.sum(jnp.where(column, found[c], 0.0), axis=0, keepdims=True) * weight[...]
        for c in range(3)
    ]
    row = lax.broadcasted_iota(jnp.int32, (8, ROWS), 0) >> 1
    pattern = jnp.where(
        row == 0, sampled[0], jnp.where(row == 1, sampled[1], jnp.where(row == 2, sampled[2], 0.0))
    )
    match, hot_lane = element_keys(dest[...], elem[...])
    spread = jnp.where(match, pattern[None], 0.0).reshape(256, ROWS)
    out[...] = put(spread, hot_lane).reshape(32, 8, 128)


def own_kernel(place, motion, coef, out):
    gx, gy = place[0], place[1]
    row = lax.broadcasted_iota(jnp.int32, (8, 128), 0)
    lane = lax.broadcasted_iota(jnp.int32, (8, 128), 1)
    level = row >> 1
    held = jnp.where(
        level == 0,
        motion[0:1, :],
        jnp.where(level == 1, motion[1:2, :], jnp.where(level == 2, motion[2:3, :], coef[...])),
    )
    moved = pltpu.roll(held, ((gx & 7) * 16 - gy * 16 + 128) & 127, 1)
    mine = ((lane >> 4) == (gx & 7)) & ((row & 1) == (gx >> 3))
    out[...] = jnp.where(mine, moved, 0.0)


def total_kernel(parts, own, out):
    total = jnp.sum(parts[...], axis=0) + own[...]
    out[...] = jnp.broadcast_to(total[None], (16, 8, 128))


def force_kernel(parts, out):
    total = jnp.sum(parts[...], axis=0)
    row = lax.broadcasted_iota(jnp.int32, (8, 128), 0)

    def by_parity(values):
        values = values + pltpu.roll(values, 4, 0)
        return values + pltpu.roll(values, 2, 0)

    speed = jnp.sqrt(by_parity(jnp.where(row < 6, total * total, 0.0)))
    coef = by_parity(jnp.where(row < 6, 0.0, total))
    force = jnp.where(row < 6, -coef * speed * total, 0.0)
    out[...] = jnp.broadcast_to(force[None], (32, 8, 128))


def spread_kernel(forces, cell, dest, elem, weight, before, new_state, body_force):
    match, hot_lane = element_keys(dest[...], elem[...])
    found = pick(forces[...].reshape(256, 128), hot_lane).reshape(32, 8, ROWS)
    pairs = jnp.sum(jnp.where(match, found, 0.0), axis=0)
    column, hot_z = cell_keys(cell[...])
    each = [(pairs[2 * c : 2 * c + 1] + pairs[2 * c + 1 : 2 * c + 2]) * weight[...] for c in range(3)]
    spread = jnp.concatenate([jnp.where(column, each[c], 0.0) for c in range(3)], axis=0)
    body = put(spread, hot_z).reshape(3, 8, 8, 128)
    body_force[...] = body
    new_state[0:3] = before[0:3] + DT_STEP * body
    new_state[3] = before[3]


def fill(grid, state, xlo, xhi, ylo, yhi):
    grid[:, 2:10, 0:8, 0:128] = state[...]
    grid[:, 0:2, 0:8, 0:128] = xlo[...]
    grid[:, 10:12, 0:8, 0:128] = xhi[...]
    grid[:, 1:11, 8:10, 0:128] = yhi[...]
    grid[:, 1:11, 14:16, 0:128] = ylo[...]


def ends_kernel(state, xlo, xhi, ylo, yhi, zup, zdown, grid):
    grid[:, :, 8:16, 0:128] = jnp.zeros((4, 12, 8, 128), jnp.float32)
    fill(grid, state, xlo, xhi, ylo, yhi)
    rows = grid[:, 1:11, :, 0:128].reshape(640, 128)
    row = lax.broadcasted_iota(jnp.int32, (8, 128), 0)
    lane = lax.broadcasted_iota(jnp.int32, (8, 128), 1)
    wanted = jnp.where(row < 2, row, jnp.where(row < 4, row + 124, -1))
    ends = lax.dot_general(
        jnp.where(lane == wanted, 1.0, 0.0),
        rows,
        (((1,), (1,)), ((), ())),
        precision=lax.Precision.HIGHEST,
        preferred_element_type=jnp.float32,
    )
    zdown[...] = ends[0:2]
    zup[...] = ends[2:4]


def stencil_kernel(place, state, xlo, xhi, ylo, yhi, zlo, zhi, out, grid):
    gz = place[2]
    fill(grid, state, xlo, xhi, ylo, yhi)
    row = lax.broadcasted_iota(jnp.int32, (4, 128), 0)
    lane = lax.broadcasted_iota(jnp.int32, (4, 128), 1)
    wanted = jnp.where(row < 2, row, row + 124)
    ghosts = lax.dot_general(
        jnp.concatenate([zhi[...], zlo[...]], axis=0),
        jnp.where(lane == wanted, 1.0, 0.0),
        (((0,), (0,)), ((), ())),
        precision=lax.Precision.HIGHEST,
        preferred_element_type=jnp.float32,
    ).reshape(4, 10, 16, 128)
    level = lax.broadcasted_iota(jnp.int32, (1, 1, 256), 2)
    outside = ((level >= 128) & (level < 192) & (gz == 3)) | ((level >= 192) & (gz == 0))
    grid[:, 1:11, :, 128:256] = jnp.where(outside[None, :, :, 128:256], 0.0, ghosts)

    def around(values):
        return (
            (pltpu.roll(values, 15, 1), pltpu.roll(values, 1, 1)),
            (pltpu.roll(values, 255, 2), pltpu.roll(values, 1, 2)),
        )

    fields = [grid[c] for c in range(4)]
    sides = []
    diffs = []
    for c in range(4):
        middle = fields[c][1:11]
        near = ((fields[c][2:12], fields[c][0:10]),) + around(middle)
        sides.append(near)
        diffs.append([upper - lower for upper, lower in near])
    strain = 0.5 * (
        diffs[0][0] * diffs[0][0] + diffs[1][1] * diffs[1][1] + diffs[2][2] * diffs[2][2]
    )
    for i, j in ((0, 1), (0, 2), (1, 2)):
        paired = diffs[i][j] + diffs[j][i]
        strain = strain + 0.25 * paired * paired
    eddy = jnp.where(outside, 0.0, SMAG_COEF * jnp.sqrt(strain))

    def inner(values):
        return values[:, 0:8, 0:128]

    centre = inner(eddy[1:9])
    near = ((eddy[2:10], eddy[0:8]),) + around(eddy[1:9])
    faces = [[0.5 * (centre + inner(side)) for side in pair] for pair in near]
    wind = [0.5 * inner(fields[c][2:10]) for c in range(3)]
    for c in range(4):
        middle = inner(fields[c][2:10])
        ratio = 1.0 if c < 3 else 1.0 / PRANDTL
        change = 0.0
        for j in range(3):
            upper, lower = [inner(side[1:9]) for side in sides[c][j]]
            change = change + (BASE_COEF + ratio * faces[j][0]) * (upper - middle)
            change = change - (BASE_COEF + ratio * faces[j][1]) * (middle - lower)
            change = change - wind[j] * (upper - lower)
        out[c] = middle + DT_STEP * change


def swap(up, down, axis):
    count = lax.axis_size(axis)
    forward = [(i, (i + 1) % count) for i in range(count)]
    backward = [(target, source) for source, target in forward]
    return lax.ppermute(up, axis, forward), lax.ppermute(down, axis, backward)


def exchange(blocks, axes):
    return lax.all_to_all(blocks, axes, split_axis=0, concat_axis=0, tiled=True)


def body(state, sample_cell, sample_dest, sample_weight, sample_elem, element_motion, element_coef):
    place = jnp.stack([lax.axis_index(axis) for axis in ("gx", "gy", "gz")]).astype(jnp.int32)
    cell = sample_cell.reshape(1, ROWS)
    dest = sample_dest.reshape(1, ROWS)
    elem = sample_elem.reshape(1, ROWS)
    weight = sample_weight.reshape(1, ROWS)

    xlo, xhi = swap(state[:, 6:8], state[:, 0:2], "gx")
    rows = pltpu.VMEM((1, ROWS), jnp.int32)
    held = (
        pltpu.VMEM((3, 8, 8, 128), jnp.float32),
        rows,
        rows,
        rows,
        pltpu.VMEM((1, ROWS), jnp.float32),
        pltpu.SemaphoreType.DMA((5,)),
    )
    partial = call(sample_kernel, f32(32, 8, 128), held, count=5, space=pltpu.HBM)(
        state, cell, dest, elem, weight
    )
    partial = exchange(partial, PLANE)
    own = call(own_kernel, f32(8, 128), smem=1, count=3)(
        place, element_motion, element_coef.reshape(1, 128)
    )
    partial, own, xlo, xhi = lax.optimization_barrier((partial, own, xlo, xhi))

    totals = call(total_kernel, f32(16, 8, 128), count=2)(partial, own)
    totals = exchange(totals, "gx")
    wide = jnp.concatenate([xlo[:, 1:2], state, xhi[:, 0:1]], axis=1)
    ylo, yhi = swap(wide[:, :, 6:8], wide[:, :, 0:2], "gy")
    totals, ylo, yhi = lax.optimization_barrier((totals, ylo, yhi))

    forces = call(force_kernel, f32(32, 8, 128), count=1)(totals)
    forces = exchange(forces, PLANE)
    padded = pltpu.VMEM((4, 12, 16, 256), jnp.float32)
    zup, zdown = call(ends_kernel, (f32(2, 640), f32(2, 640)), (padded,), count=5)(
        state, xlo, xhi, ylo, yhi
    )
    zlo, zhi = swap(zup, zdown, "gz")

    before = call(stencil_kernel, f32(4, 8, 8, 128), (padded,), smem=1, count=8)(
        place, state, xlo, xhi, ylo, yhi, zlo, zhi
    )
    return call(spread_kernel, (f32(4, 8, 8, 128), f32(3, 8, 8, 128)), count=6)(
        forces, cell, dest, elem, weight, before
    )


def solution(mesh):
    return jax.shard_map(
        body,
        mesh=mesh,
        in_specs=(
            P(None, "gx", "gy", "gz"),
            P(("gx", "gy", "gz")),
            P(("gx", "gy", "gz"), None),
            P(("gx", "gy", "gz")),
            P(("gx", "gy", "gz")),
            P(None, ("gx", "gz")),
            P(("gx", "gz")),
        ),
        out_specs=(P(None, "gx", "gy", "gz"), P(None, "gx", "gy", "gz")),
        check_vma=False,
    )
```

```python
import jax
import jax.numpy as jnp
from jax import lax
from jax.experimental import pallas as pl
from jax.experimental.pallas import tpu as pltpu
from jax.sharding import PartitionSpec as P

DT_STEP = 0.4
BASE_COEF = 0.02
PRANDTL = 0.7
SMAG_COEF = 0.04

ROWS = 1024
PLANE = ("gy", "gz")


def call(kernel, outs, scratch=(), count=1, space=pltpu.VMEM, limit=24 * 1024 * 1024):
    return pl.pallas_call(
        kernel,
        out_shape=outs,
        in_specs=[pl.BlockSpec(memory_space=space)] * count,
        out_specs=jax.tree.map(lambda _: pl.BlockSpec(memory_space=pltpu.VMEM), outs),
        scratch_shapes=scratch,
        compiler_params=pltpu.CompilerParams(vmem_limit_bytes=limit),
        cost_estimate=pl.CostEstimate(
            flops=2_000_000, bytes_accessed=1_000_000, transcendentals=0
        ),
    )


def f32(*shape):
    return jax.ShapeDtypeStruct(shape, jnp.float32)


def halves(values):
    high = values.astype(jnp.bfloat16)
    return high, (values - high.astype(jnp.float32)).astype(jnp.bfloat16)


def onehot(index, size):
    wanted = lax.broadcasted_iota(jnp.int32, (size, ROWS), 0)
    return jnp.where(wanted == index, 1.0, 0.0).astype(jnp.bfloat16)


def pick(table, hot):
    both = jnp.concatenate(halves(table), axis=1)
    return jnp.dot(both, jnp.concatenate([hot, hot], axis=0), preferred_element_type=jnp.float32)


def put(values, hot):
    high, low = halves(values)
    dims = (((1,), (1,)), ((), ()))
    total = lax.dot_general(high, hot, dims, preferred_element_type=jnp.float32)
    return total + lax.dot_general(low, hot, dims, preferred_element_type=jnp.float32)


def cell_keys(cell):
    column = lax.broadcasted_iota(jnp.int32, (64, ROWS), 0) == (cell >> 7)
    return column, onehot(cell & 127, 128)


def element_keys(dest, elem):
    tile = (elem >> 4) * 4 + (dest & 3)
    along = dest >> 2
    number = tile * 2 + (along >> 3)
    shape = (32, 8, ROWS)
    row = lax.broadcasted_iota(jnp.int32, shape, 0) * 2 + (
        lax.broadcasted_iota(jnp.int32, shape, 1) & 1
    )
    return row == number[None], onehot((along & 7) * 16 + (elem & 15), 128)


def own_part(motion, coef):
    gx, gy = lax.axis_index("gx"), lax.axis_index("gy")
    row = lax.broadcasted_iota(jnp.int32, (8, 128), 0)
    lane = lax.broadcasted_iota(jnp.int32, (8, 128), 1)
    level = row >> 1
    held = jnp.where(
        level == 0,
        motion[0:1, :],
        jnp.where(level == 1, motion[1:2, :], jnp.where(level == 2, motion[2:3, :], coef[...])),
    )
    moved = pltpu.roll(held, ((gx & 7) * 16 - gy * 16 + 128) & 127, 1)
    mine = ((lane >> 4) == (gx & 7)) & ((row & 1) == (gx >> 3))
    return jnp.where(mine, moved, 0.0)


def sample_kernel(
    state_in, cell_in, dest_in, elem_in, weight_in, motion_in, coef_in, out, own, *scratch
):
    held, sems = scratch[:7], scratch[7]
    sources = (state_in.at[0:3], cell_in, dest_in, elem_in, weight_in, motion_in, coef_in)
    copies = [
        pltpu.make_async_copy(source, target, sems.at[i])
        for i, (source, target) in enumerate(zip(sources, held))
    ]
    for copy in copies:
        copy.start()
    for copy in copies:
        copy.wait()
    state, cell, dest, elem, weight, motion, coef = held
    own[...] = own_part(motion, coef)
    column, hot_z = cell_keys(cell[...])
    found = pick(state[...].reshape(192, 128), hot_z).reshape(3, 64, ROWS)
    sampled = [
        jnp.sum(jnp.where(column, found[c], 0.0), axis=0, keepdims=True) * weight[...]
        for c in range(3)
    ]
    row = lax.broadcasted_iota(jnp.int32, (8, ROWS), 0) >> 1
    pattern = jnp.where(
        row == 0, sampled[0], jnp.where(row == 1, sampled[1], jnp.where(row == 2, sampled[2], 0.0))
    )
    match, hot_lane = element_keys(dest[...], elem[...])
    spread = jnp.where(match, pattern[None], 0.0).reshape(256, ROWS)
    out[...] = put(spread, hot_lane).reshape(32, 8, 128)


def total_kernel(parts, own, out):
    total = jnp.sum(parts[...], axis=0) + own[...]
    out[...] = jnp.broadcast_to(total[None], (16, 8, 128))


def force_kernel(parts, packs, out):
    total = jnp.sum(parts[...], axis=0)
    row = lax.broadcasted_iota(jnp.int32, (8, 128), 0)

    def by_parity(values):
        values = values + pltpu.roll(values, 4, 0)
        return values + pltpu.roll(values, 2, 0)

    speed = jnp.sqrt(by_parity(jnp.where(row < 6, total * total, 0.0)))
    coef = by_parity(jnp.where(row < 6, 0.0, total))
    force = jnp.where(row < 6, -coef * speed * total, 0.0)
    out[:, 0:8] = jnp.broadcast_to(force[None], (32, 8, 128))
    above = (lax.axis_index("gz") + 1) & 3
    for level in range(4):
        pack = jnp.where(above == level, packs[1], packs[0])
        for across in range(8):
            out[4 * across + level, 8:16] = pack


def fill(grid, state, xlo, xhi, ylo, yhi):
    grid[:, 2:10, 0:8, 0:128] = state[...]
    grid[:, 0:2, 0:8, 0:128] = xlo[...]
    grid[:, 10:12, 0:8, 0:128] = xhi[...]
    grid[:, 1:11, 8:10, 0:128] = yhi[...]
    grid[:, 1:11, 14:16, 0:128] = ylo[...]


def lanes(count, places):
    row = lax.broadcasted_iota(jnp.int32, (count, 128), 0)
    lane = lax.broadcasted_iota(jnp.int32, (count, 128), 1)
    hot = (row == 0) & (lane == places[0])
    for i, place in enumerate(places[1:]):
        hot = hot | ((row == i + 1) & (lane == place))
    return jnp.where(hot, 1.0, 0.0)


def exact(left, right, dims):
    return lax.dot_general(
        left,
        right,
        ((dims, dims), ((), ())),
        precision=lax.Precision.HIGHEST,
        preferred_element_type=jnp.float32,
    )


def ends_kernel(state, xlo, xhi, ylo, yhi, packs, grid):
    grid[:, :, 8:16] = jnp.zeros((4, 12, 8, 128), jnp.float32)
    fill(grid, state, xlo, xhi, ylo, yhi)
    near = exact(lanes(8, (0, 127)), grid[:, 1:11].reshape(640, 128), (1,))
    far = exact(lanes(8, (1, 126)), state[...].reshape(256, 128), (1,))
    for side in range(2):
        pieces = [near[side : side + 1, 128 * i : 128 * i + 128] for i in range(5)]
        pieces += [far[side : side + 1, 128 * i : 128 * i + 128] for i in range(2)]
        packs[side] = jnp.concatenate(pieces + [jnp.zeros((1, 128), jnp.float32)], axis=0)


def unpack(high, low):
    def rows(pack, first, count):
        return jnp.concatenate([pack[i : i + 1] for i in range(first, first + count)], axis=1)

    near = jnp.concatenate([rows(high, 0, 5), rows(low, 0, 5)], axis=0)
    far = jnp.concatenate([rows(high, 5, 2), rows(low, 5, 2)], axis=0)
    near = exact(near, lanes(2, (0, 127)), (0,)).reshape(4, 10, 16, 128)
    return near, exact(far, lanes(2, (1, 126)), (0,)).reshape(4, 8, 8, 128)


def final_kernel(
    parts, cell, dest, elem, weight, state, xlo, xhi, ylo, yhi, new_state, body_force, grid
):
    match, hot_lane = element_keys(dest[...], elem[...])
    found = pick(parts[:, 0:8].reshape(256, 128), hot_lane).reshape(32, 8, ROWS)
    pairs = jnp.sum(jnp.where(match, found, 0.0), axis=0)
    column, hot_z = cell_keys(cell[...])
    each = [(pairs[2 * c : 2 * c + 1] + pairs[2 * c + 1 : 2 * c + 2]) * weight[...] for c in range(3)]
    spread = jnp.concatenate([jnp.where(column, each[c], 0.0) for c in range(3)], axis=0)
    body = put(spread, hot_z).reshape(3, 8, 8, 128)
    body_force[...] = body

    gy, gz = lax.axis_index("gy"), lax.axis_index("gz")
    fill(grid, state, xlo, xhi, ylo, yhi)
    near, far = unpack(parts[gy * 4 + ((gz + 1) & 3), 8:16], parts[gy * 4 + ((gz + 3) & 3), 8:16])
    level = lax.broadcasted_iota(jnp.int32, (1, 1, 256), 2)
    outside = ((level >= 128) & (level < 192) & (gz == 3)) | ((level >= 192) & (gz == 0))
    beyond = outside[:, :, 128:256][None]
    grid[:, 1:11, :, 128:256] = jnp.where(beyond, 0.0, near)
    grid[:, 2:10, 0:8, 128:256] += jnp.where(beyond, 0.0, far)

    def around(values):
        return (
            (pltpu.roll(values, 15, 1), pltpu.roll(values, 1, 1)),
            (pltpu.roll(values, 255, 2), pltpu.roll(values, 1, 2)),
        )

    fields = [grid[c] for c in range(4)]
    sides = []
    diffs = []
    for c in range(4):
        middle = fields[c][1:11]
        near = ((fields[c][2:12], fields[c][0:10]),) + around(middle)
        sides.append(near)
        diffs.append([upper - lower for upper, lower in near])
    strain = 0.5 * (
        diffs[0][0] * diffs[0][0] + diffs[1][1] * diffs[1][1] + diffs[2][2] * diffs[2][2]
    )
    for i, j in ((0, 1), (0, 2), (1, 2)):
        paired = diffs[i][j] + diffs[j][i]
        strain = strain + 0.25 * paired * paired
    eddy = jnp.where(outside, 0.0, SMAG_COEF * jnp.sqrt(strain))

    def inner(values):
        return values[:, 0:8, 0:128]

    centre = inner(eddy[1:9])
    near = ((eddy[2:10], eddy[0:8]),) + around(eddy[1:9])
    faces = [[0.5 * (centre + inner(side)) for side in pair] for pair in near]
    wind = [0.5 * inner(fields[c][2:10]) for c in range(3)]
    for c in range(4):
        middle = inner(fields[c][2:10])
        ratio = 1.0 if c < 3 else 1.0 / PRANDTL
        change = 0.0
        for j in range(3):
            upper, lower = [inner(side[1:9]) for side in sides[c][j]]
            change = change + (BASE_COEF + ratio * faces[j][0]) * (upper - middle)
            change = change - (BASE_COEF + ratio * faces[j][1]) * (middle - lower)
            change = change - wind[j] * (upper - lower)
        if c < 3:
            change = change + body[c]
        new_state[c] = middle + DT_STEP * change


def swap(up, down, axis):
    count = lax.axis_size(axis)
    forward = [(i, (i + 1) % count) for i in range(count)]
    backward = [(target, source) for source, target in forward]
    return lax.ppermute(up, axis, forward), lax.ppermute(down, axis, backward)


def exchange(blocks, axes):
    return lax.all_to_all(blocks, axes, split_axis=0, concat_axis=0, tiled=True)


def body(state, sample_cell, sample_dest, sample_weight, sample_elem, element_motion, element_coef):
    cell = sample_cell.reshape(1, ROWS)
    dest = sample_dest.reshape(1, ROWS)
    elem = sample_elem.reshape(1, ROWS)
    weight = sample_weight.reshape(1, ROWS)

    xlo, xhi = swap(state[:, 6:8], state[:, 0:2], "gx")
    coef = element_coef.reshape(1, 128)
    rows = pltpu.VMEM((1, ROWS), jnp.int32)
    held = (
        pltpu.VMEM((3, 8, 8, 128), jnp.float32),
        rows,
        rows,
        rows,
        pltpu.VMEM((1, ROWS), jnp.float32),
        pltpu.VMEM((3, 128), jnp.float32),
        pltpu.VMEM((1, 128), jnp.float32),
        pltpu.SemaphoreType.DMA((7,)),
    )
    partial, own = call(
        sample_kernel, (f32(32, 8, 128), f32(8, 128)), held, 7, pltpu.HBM, 60 * 1024 * 1024
    )(state, cell, dest, elem, weight, element_motion, coef)
    partial = exchange(partial, PLANE)
    partial, own, xlo, xhi = lax.optimization_barrier((partial, own, xlo, xhi))

    totals = call(total_kernel, f32(16, 8, 128), count=2)(partial, own)
    totals = exchange(totals, "gx")
    wide = jnp.concatenate([xlo[:, 1:2], state, xhi[:, 0:1]], axis=1)
    ylo, yhi = swap(wide[:, :, 6:8], wide[:, :, 0:2], "gy")
    ghosts = (xlo, xhi, ylo, yhi)
    packs = call(ends_kernel, f32(2, 8, 128), (pltpu.VMEM((4, 12, 16, 128), jnp.float32),), 5)(
        state, *ghosts
    )

    forces = call(force_kernel, f32(32, 16, 128), count=2)(totals, packs)
    forces = exchange(forces, PLANE)
    grid = pltpu.VMEM((4, 12, 16, 256), jnp.float32)
    return call(final_kernel, (f32(4, 8, 8, 128), f32(3, 8, 8, 128)), (grid,), 10)(
        forces, cell, dest, elem, weight, state, *ghosts
    )


def solution(mesh):
    return jax.shard_map(
        body,
        mesh=mesh,
        in_specs=(
            P(None, "gx", "gy", "gz"),
            P(("gx", "gy", "gz")),
            P(("gx", "gy", "gz"), None),
            P(("gx", "gy", "gz")),
            P(("gx", "gy", "gz")),
            P(None, ("gx", "gz")),
            P(("gx", "gz")),
        ),
        out_specs=(P(None, "gx", "gy", "gz"), P(None, "gx", "gy", "gz")),
        check_vma=False,
    )
```

```python
import jax
import jax.numpy as jnp
from jax import lax
from jax.experimental import pallas as pl
from jax.experimental.pallas import tpu as pltpu
from jax.sharding import PartitionSpec as P

DT_STEP = 0.4
BASE_COEF = 0.02
PRANDTL = 0.7
SMAG_COEF = 0.04

ROWS = 1024
PLANE = ("gy", "gz")


def call(kernel, outs, scratch=(), count=1, space=pltpu.VMEM, limit=24 * 1024 * 1024):
    return pl.pallas_call(
        kernel,
        out_shape=outs,
        in_specs=[pl.BlockSpec(memory_space=space)] * count,
        out_specs=jax.tree.map(lambda _: pl.BlockSpec(memory_space=pltpu.VMEM), outs),
        scratch_shapes=scratch,
        compiler_params=pltpu.CompilerParams(vmem_limit_bytes=limit),
        cost_estimate=pl.CostEstimate(
            flops=2_000_000, bytes_accessed=1_000_000, transcendentals=0
        ),
    )


def f32(*shape):
    return jax.ShapeDtypeStruct(shape, jnp.float32)


def halves(values):
    high = values.astype(jnp.bfloat16)
    return high, (values - high.astype(jnp.float32)).astype(jnp.bfloat16)


def onehot(index, size):
    wanted = lax.broadcasted_iota(jnp.int32, (size, ROWS), 0)
    return jnp.where(wanted == index, 1.0, 0.0).astype(jnp.bfloat16)


def pick(table, hot):
    both = jnp.concatenate(halves(table), axis=1)
    return jnp.dot(both, jnp.concatenate([hot, hot], axis=0), preferred_element_type=jnp.float32)


def put(values, hot):
    high, low = halves(values)
    dims = (((1,), (1,)), ((), ()))
    total = lax.dot_general(high, hot, dims, preferred_element_type=jnp.float32)
    return total + lax.dot_general(low, hot, dims, preferred_element_type=jnp.float32)


def cell_keys(cell):
    column = lax.broadcasted_iota(jnp.int32, (64, ROWS), 0) == (cell >> 7)
    return column, onehot(cell & 127, 128)


def element_keys(dest, elem):
    tile = (elem >> 4) * 4 + (dest & 3)
    along = dest >> 2
    number = tile * 2 + (along >> 3)
    shape = (32, 8, ROWS)
    row = lax.broadcasted_iota(jnp.int32, shape, 0) * 2 + (
        lax.broadcasted_iota(jnp.int32, shape, 1) & 1
    )
    return row == number[None], onehot((along & 7) * 16 + (elem & 15), 128)


def own_part(motion, coef):
    gx, gy = lax.axis_index("gx"), lax.axis_index("gy")
    row = lax.broadcasted_iota(jnp.int32, (8, 128), 0)
    lane = lax.broadcasted_iota(jnp.int32, (8, 128), 1)
    level = row >> 1
    held = jnp.where(
        level == 0,
        motion[0:1, :],
        jnp.where(level == 1, motion[1:2, :], jnp.where(level == 2, motion[2:3, :], coef[...])),
    )
    moved = pltpu.roll(held, ((gx & 7) * 16 - gy * 16 + 128) & 127, 1)
    mine = ((lane >> 4) == (gx & 7)) & ((row & 1) == (gx >> 3))
    return jnp.where(mine, moved, 0.0)


def lanes(count, places):
    row = lax.broadcasted_iota(jnp.int32, (count, 128), 0)
    lane = lax.broadcasted_iota(jnp.int32, (count, 128), 1)
    hot = (row == 0) & (lane == places[0])
    for i, place in enumerate(places[1:]):
        hot = hot | ((row == i + 1) & (lane == place))
    return jnp.where(hot, 1.0, 0.0)


def exact(left, right, dims):
    return lax.dot_general(
        left,
        right,
        ((dims, dims), ((), ())),
        precision=lax.Precision.HIGHEST,
        preferred_element_type=jnp.float32,
    )


def sample_kernel(
    state_in,
    cell_in,
    dest_in,
    elem_in,
    weight_in,
    motion_in,
    coef_in,
    out,
    own,
    yup,
    ydown,
    *scratch,
):
    held, sems = scratch[:7], scratch[7]
    sources = (state_in, cell_in, dest_in, elem_in, weight_in, motion_in, coef_in)
    copies = [
        pltpu.make_async_copy(source, target, sems.at[i])
        for i, (source, target) in enumerate(zip(sources, held))
    ]
    for copy in copies:
        copy.start()
    for copy in copies:
        copy.wait()
    state, cell, dest, elem, weight, motion, coef = held
    own[...] = own_part(motion, coef)
    yup[...] = state[:, :, 6:8]
    ydown[...] = state[:, :, 0:2]
    ends = exact(lanes(8, (0, 127, 1, 126)), state[...].reshape(256, 128), (1,))
    pack = [ends[i : i + 1, 128 * j : 128 * j + 128] for i in range(4) for j in range(2)]
    out[:, 8:16] = jnp.broadcast_to(jnp.concatenate(pack, axis=0)[None], (32, 8, 128))
    column, hot_z = cell_keys(cell[...])
    found = pick(state[0:3].reshape(192, 128), hot_z).reshape(3, 64, ROWS)
    sampled = [
        jnp.sum(jnp.where(column, found[c], 0.0), axis=0, keepdims=True) * weight[...]
        for c in range(3)
    ]
    row = lax.broadcasted_iota(jnp.int32, (8, ROWS), 0) >> 1
    pattern = jnp.where(
        row == 0, sampled[0], jnp.where(row == 1, sampled[1], jnp.where(row == 2, sampled[2], 0.0))
    )
    match, hot_lane = element_keys(dest[...], elem[...])
    spread = jnp.where(match, pattern[None], 0.0).reshape(256, ROWS)
    out[:, 0:8] = put(spread, hot_lane).reshape(32, 8, 128)


def total_kernel(parts, own, out):
    total = jnp.sum(parts[:, 0:8], axis=0) + own[...]
    out[...] = jnp.broadcast_to(total[None], (16, 8, 128))


def force_kernel(parts, out):
    total = jnp.sum(parts[...], axis=0)
    row = lax.broadcasted_iota(jnp.int32, (8, 128), 0)

    def by_parity(values):
        values = values + pltpu.roll(values, 4, 0)
        return values + pltpu.roll(values, 2, 0)

    speed = jnp.sqrt(by_parity(jnp.where(row < 6, total * total, 0.0)))
    coef = by_parity(jnp.where(row < 6, 0.0, total))
    force = jnp.where(row < 6, -coef * speed * total, 0.0)
    out[...] = jnp.broadcast_to(force[None], (32, 8, 128))


def fill(grid, state, ylo, yhi, ghosts, first, second):
    grid[:, 2:10, 0:8, 0:128] = state[...]
    grid[:, 2:10, 8:10, 0:128] = yhi[...]
    grid[:, 2:10, 14:16, 0:128] = ylo[...]
    grid[:, 2:10, :, 128:256] = ghosts[...]
    even = (lax.axis_index("gx") & 1) == 0
    for plane, near, slab in (
        (0, 1, jnp.where(even, second[...], first[...])),
        (10, 10, jnp.where(even, first[...], second[...])),
    ):
        grid[:, plane : plane + 2, 0:8, 0:128] = slab[:, 0:2]
        grid[:, near, 8:16, 0:128] = slab[:, 2]
        grid[:, near, 0:8, 128:256] = slab[:, 3]


def faces_kernel(parts, state, ylo, yhi, first, second, ghosts):
    gx, gy, gz = [lax.axis_index(axis) for axis in ("gx", "gy", "gz")]
    lane = lax.broadcasted_iota(jnp.int32, (1, 256), 1)

    def rows(across, up, top):
        pack = parts[((gy + across) & 7) * 4 + ((gz + (1 if up else 3)) & 3), 8:16]
        found = jnp.concatenate([pack[top : top + 1], pack[top + 1 : top + 2]], axis=1)
        return jnp.where(gz == (3 if up else 0), 0.0, found)

    def edge(up, top):
        y = lane & 7
        beside = jnp.where(y == 0, rows(1, up, top), 0.0)
        return jnp.where(y == 7, rows(7, up, top), beside)

    inner = jnp.concatenate(
        [rows(0, True, 0), rows(0, False, 2), rows(0, True, 4), rows(0, False, 6)], axis=0
    )
    inner = exact(inner, lanes(4, (0, 127, 1, 126)), (0,)).reshape(4, 8, 8, 128)
    edges = jnp.concatenate([edge(True, 0), edge(False, 2)], axis=0)
    ghosts[:, :, 0:8] = inner
    ghosts[:, :, 8:16] = exact(edges, lanes(2, (0, 127)), (0,)).reshape(4, 8, 8, 128)

    even = (gx & 1) == 0
    row = lax.broadcasted_iota(jnp.int32, (1, 8, 128), 1)

    def slab(x, near):
        beside = jnp.where(
            row == 0, yhi[:, near, 0:1], jnp.where(row == 7, ylo[:, near, 1:2], 0.0)
        )
        return [state[:, x], state[:, x + 1], beside, inner[:, near]]

    for i, (high, low) in enumerate(zip(slab(6, 7), slab(0, 0))):
        first[:, i] = jnp.where(even, high, low)
        second[:, i] = jnp.where(even, low, high)


def final_kernel(
    parts, cell, dest, elem, weight, state, ylo, yhi, ghosts, first, second, *results
):
    new_state, body_force, grid = results
    match, hot_lane = element_keys(dest[...], elem[...])
    found = pick(parts[...].reshape(256, 128), hot_lane).reshape(32, 8, ROWS)
    pairs = jnp.sum(jnp.where(match, found, 0.0), axis=0)
    column, hot_z = cell_keys(cell[...])
    each = [(pairs[2 * c : 2 * c + 1] + pairs[2 * c + 1 : 2 * c + 2]) * weight[...] for c in range(3)]
    spread = jnp.concatenate([jnp.where(column, each[c], 0.0) for c in range(3)], axis=0)
    body = put(spread, hot_z).reshape(3, 8, 8, 128)
    body_force[...] = body

    gz = lax.axis_index("gz")
    fill(grid, state, ylo, yhi, ghosts, first, second)
    level = lax.broadcasted_iota(jnp.int32, (1, 1, 256), 2)
    outside = ((level >= 128) & (level < 192) & (gz == 3)) | ((level >= 192) & (gz == 0))

    def around(values):
        return (
            (pltpu.roll(values, 15, 1), pltpu.roll(values, 1, 1)),
            (pltpu.roll(values, 255, 2), pltpu.roll(values, 1, 2)),
        )

    fields = [grid[c] for c in range(4)]
    sides = []
    diffs = []
    for c in range(4):
        middle = fields[c][1:11]
        near = ((fields[c][2:12], fields[c][0:10]),) + around(middle)
        sides.append(near)
        diffs.append([upper - lower for upper, lower in near])
    strain = 0.5 * (
        diffs[0][0] * diffs[0][0] + diffs[1][1] * diffs[1][1] + diffs[2][2] * diffs[2][2]
    )
    for i, j in ((0, 1), (0, 2), (1, 2)):
        paired = diffs[i][j] + diffs[j][i]
        strain = strain + 0.25 * paired * paired
    eddy = jnp.where(outside, 0.0, SMAG_COEF * jnp.sqrt(strain))

    def inner(values):
        return values[:, 0:8, 0:128]

    centre = inner(eddy[1:9])
    near = ((eddy[2:10], eddy[0:8]),) + around(eddy[1:9])
    faces = [[0.5 * (centre + inner(side)) for side in pair] for pair in near]
    wind = [0.5 * inner(fields[c][2:10]) for c in range(3)]
    for c in range(4):
        middle = inner(fields[c][2:10])
        ratio = 1.0 if c < 3 else 1.0 / PRANDTL
        change = 0.0
        for j in range(3):
            upper, lower = [inner(side[1:9]) for side in sides[c][j]]
            change = change + (BASE_COEF + ratio * faces[j][0]) * (upper - middle)
            change = change - (BASE_COEF + ratio * faces[j][1]) * (middle - lower)
            change = change - wind[j] * (upper - lower)
        if c < 3:
            change = change + body[c]
        new_state[c] = middle + DT_STEP * change


def shift(up, down, axis):
    count = lax.axis_size(axis)
    forward = [(i, (i + 1) % count) for i in range(count)]
    backward = [(target, source) for source, target in forward]
    return lax.ppermute(up, axis, forward), lax.ppermute(down, axis, backward)


def swap(slab, axis, odd):
    count = lax.axis_size(axis)
    return lax.ppermute(
        slab, axis, [(i, (i + 1 if i % 2 == odd else i - 1) % count) for i in range(count)]
    )


def exchange(blocks, axes):
    return lax.all_to_all(blocks, axes, split_axis=0, concat_axis=0, tiled=True)


def body(state, sample_cell, sample_dest, sample_weight, sample_elem, element_motion, element_coef):
    cell = sample_cell.reshape(1, ROWS)
    dest = sample_dest.reshape(1, ROWS)
    elem = sample_elem.reshape(1, ROWS)
    weight = sample_weight.reshape(1, ROWS)

    coef = element_coef.reshape(1, 128)
    rows = pltpu.VMEM((1, ROWS), jnp.int32)
    held = (
        pltpu.VMEM((4, 8, 8, 128), jnp.float32),
        rows,
        rows,
        rows,
        pltpu.VMEM((1, ROWS), jnp.float32),
        pltpu.VMEM((3, 128), jnp.float32),
        pltpu.VMEM((1, 128), jnp.float32),
        pltpu.SemaphoreType.DMA((7,)),
    )
    side = f32(4, 8, 2, 128)
    partial, own, yup, ydown = call(
        sample_kernel,
        (f32(32, 16, 128), f32(8, 128), side, side),
        held,
        7,
        pltpu.HBM,
        60 * 1024 * 1024,
    )(state, cell, dest, elem, weight, element_motion, coef)
    parts = exchange(partial, PLANE)
    ylo, yhi = shift(yup, ydown, "gy")
    parts, ylo, yhi = lax.optimization_barrier((parts, ylo, yhi))

    totals = call(total_kernel, f32(16, 8, 128), count=2)(parts, own)
    totals = exchange(totals, "gx")
    slab = f32(4, 4, 8, 128)
    first, second, ghosts = call(faces_kernel, (slab, slab, f32(4, 8, 16, 128)), count=4)(
        parts, state, ylo, yhi
    )
    first = swap(first, "gx", 0)
    totals, first = lax.optimization_barrier((totals, first))

    forces = call(force_kernel, f32(32, 8, 128), count=1)(totals)
    forces, second = lax.optimization_barrier((forces, second))
    forces = exchange(forces, PLANE)
    second = swap(second, "gx", 1)
    grid = pltpu.VMEM((4, 12, 16, 256), jnp.float32)
    return call(final_kernel, (f32(4, 8, 8, 128), f32(3, 8, 8, 128)), (grid,), 11)(
        forces, cell, dest, elem, weight, state, ylo, yhi, ghosts, first, second
    )


def solution(mesh):
    return jax.shard_map(
        body,
        mesh=mesh,
        in_specs=(
            P(None, "gx", "gy", "gz"),
            P(("gx", "gy", "gz")),
            P(("gx", "gy", "gz"), None),
            P(("gx", "gy", "gz")),
            P(("gx", "gy", "gz")),
            P(None, ("gx", "gz")),
            P(("gx", "gz")),
        ),
        out_specs=(P(None, "gx", "gy", "gz"), P(None, "gx", "gy", "gz")),
        check_vma=False,
    )
```

```python
import jax
import jax.numpy as jnp
from jax import lax
from jax.experimental import pallas as pl
from jax.experimental.pallas import tpu as pltpu
from jax.sharding import PartitionSpec as P

DT_STEP = 0.4
BASE_COEF = 0.02
PRANDTL = 0.7
SMAG_COEF = 0.04

ROWS = 1024
PLANE = ("gy", "gz")


def call(kernel, outs, scratch=(), count=1, space=pltpu.VMEM, limit=24 * 1024 * 1024):
    return pl.pallas_call(
        kernel,
        out_shape=outs,
        in_specs=[pl.BlockSpec(memory_space=space)] * count,
        out_specs=jax.tree.map(lambda _: pl.BlockSpec(memory_space=pltpu.VMEM), outs),
        scratch_shapes=scratch,
        compiler_params=pltpu.CompilerParams(vmem_limit_bytes=limit),
        cost_estimate=pl.CostEstimate(
            flops=2_000_000, bytes_accessed=1_000_000, transcendentals=0
        ),
    )


def f32(*shape):
    return jax.ShapeDtypeStruct(shape, jnp.float32)


def halves(values):
    high = values.astype(jnp.bfloat16)
    return high, (values - high.astype(jnp.float32)).astype(jnp.bfloat16)


def onehot(index, size):
    wanted = lax.broadcasted_iota(jnp.int32, (size, ROWS), 0)
    return jnp.where(wanted == index, 1.0, 0.0).astype(jnp.bfloat16)


def pick(table, hot):
    both = jnp.concatenate(halves(table), axis=1)
    return jnp.dot(both, jnp.concatenate([hot, hot], axis=0), preferred_element_type=jnp.float32)


def put(values, hot):
    high, low = halves(values)
    dims = (((1,), (1,)), ((), ()))
    total = lax.dot_general(high, hot, dims, preferred_element_type=jnp.float32)
    return total + lax.dot_general(low, hot, dims, preferred_element_type=jnp.float32)


def cell_keys(cell):
    column = lax.broadcasted_iota(jnp.int32, (64, ROWS), 0) == (cell >> 7)
    return column, onehot(cell & 127, 128)


def element_keys(dest, elem):
    tile = (elem >> 4) * 4 + (dest & 3)
    along = dest >> 2
    number = tile * 2 + (along >> 3)
    shape = (32, 8, ROWS)
    row = lax.broadcasted_iota(jnp.int32, shape, 0) * 2 + (
        lax.broadcasted_iota(jnp.int32, shape, 1) & 1
    )
    return row == number[None], onehot((along & 7) * 16 + (elem & 15), 128)


def own_part(motion, coef):
    gx, gy = lax.axis_index("gx"), lax.axis_index("gy")
    row = lax.broadcasted_iota(jnp.int32, (8, 128), 0)
    lane = lax.broadcasted_iota(jnp.int32, (8, 128), 1)
    level = row >> 1
    held = jnp.where(
        level == 0,
        motion[0:1, :],
        jnp.where(level == 1, motion[1:2, :], jnp.where(level == 2, motion[2:3, :], coef[...])),
    )
    moved = pltpu.roll(held, ((gx & 7) * 16 - gy * 16 + 128) & 127, 1)
    mine = ((lane >> 4) == (gx & 7)) & ((row & 1) == (gx >> 3))
    return jnp.where(mine, moved, 0.0)


def lanes(count, places):
    row = lax.broadcasted_iota(jnp.int32, (count, 128), 0)
    lane = lax.broadcasted_iota(jnp.int32, (count, 128), 1)
    hot = (row == 0) & (lane == places[0])
    for i, place in enumerate(places[1:]):
        hot = hot | ((row == i + 1) & (lane == place))
    return jnp.where(hot, 1.0, 0.0)


def exact(left, right, dims):
    return lax.dot_general(
        left,
        right,
        ((dims, dims), ((), ())),
        precision=lax.Precision.HIGHEST,
        preferred_element_type=jnp.float32,
    )


def sample_kernel(
    state_in,
    cell_in,
    dest_in,
    elem_in,
    weight_in,
    motion_in,
    coef_in,
    out,
    own,
    yup,
    ydown,
    *scratch,
):
    held, sems = scratch[:7], scratch[7]
    sources = (state_in, cell_in, dest_in, elem_in, weight_in, motion_in, coef_in)
    copies = [
        pltpu.make_async_copy(source, target, sems.at[i])
        for i, (source, target) in enumerate(zip(sources, held))
    ]
    for copy in copies:
        copy.start()
    for copy in copies:
        copy.wait()
    state, cell, dest, elem, weight, motion, coef = held
    own[...] = own_part(motion, coef)
    yup[...] = state[:, :, 6:8]
    ydown[...] = state[:, :, 0:2]
    ends = exact(lanes(8, (0, 127, 1, 126)), state[...].reshape(256, 128), (1,))
    pack = [ends[i : i + 1, 128 * j : 128 * j + 128] for i in range(4) for j in range(2)]
    out[:, 8:16] = jnp.broadcast_to(jnp.concatenate(pack, axis=0)[None], (32, 8, 128))
    column, hot_z = cell_keys(cell[...])
    found = pick(state[0:3].reshape(192, 128), hot_z).reshape(3, 64, ROWS)
    sampled = [
        jnp.sum(jnp.where(column, found[c], 0.0), axis=0, keepdims=True) * weight[...]
        for c in range(3)
    ]
    row = lax.broadcasted_iota(jnp.int32, (8, ROWS), 0) >> 1
    pattern = jnp.where(
        row == 0, sampled[0], jnp.where(row == 1, sampled[1], jnp.where(row == 2, sampled[2], 0.0))
    )
    match, hot_lane = element_keys(dest[...], elem[...])
    spread = jnp.where(match, pattern[None], 0.0).reshape(256, ROWS)
    out[:, 0:8] = put(spread, hot_lane).reshape(32, 8, 128)


def total_kernel(parts, own, out):
    total = jnp.sum(parts[:, 0:8], axis=0) + own[...]
    out[...] = jnp.broadcast_to(total[None], (16, 8, 128))


def force_kernel(parts, out):
    total = jnp.sum(parts[...], axis=0)
    row = lax.broadcasted_iota(jnp.int32, (8, 128), 0)

    def by_parity(values):
        values = values + pltpu.roll(values, 4, 0)
        return values + pltpu.roll(values, 2, 0)

    speed = jnp.sqrt(by_parity(jnp.where(row < 6, total * total, 0.0)))
    coef = by_parity(jnp.where(row < 6, 0.0, total))
    force = jnp.where(row < 6, -coef * speed * total, 0.0)
    out[...] = jnp.broadcast_to(force[None], (32, 8, 128))


def fill(grid, state, ylo, yhi, ghosts, first, second):
    grid[:, 2:10, 0:8, 0:128] = state[...]
    grid[:, 2:10, 8:10, 0:128] = yhi[...]
    grid[:, 2:10, 14:16, 0:128] = ylo[...]
    grid[:, 2:10, :, 128:256] = ghosts[...]
    even = (lax.axis_index("gx") & 1) == 0
    for plane, near, slab in (
        (0, 1, jnp.where(even, second[...], first[...])),
        (10, 10, jnp.where(even, first[...], second[...])),
    ):
        grid[:, plane : plane + 2, 0:8, 0:128] = slab[:, 0:2]
        grid[:, near, 8:16, 0:128] = slab[:, 2]
        grid[:, near, 0:8, 128:256] = slab[:, 3]


def faces_kernel(parts, state, ylo, yhi, first, second, ghosts):
    gx, gy, gz = [lax.axis_index(axis) for axis in ("gx", "gy", "gz")]
    lane = lax.broadcasted_iota(jnp.int32, (1, 256), 1)

    def rows(across, up, top):
        pack = parts[((gy + across) & 7) * 4 + ((gz + (1 if up else 3)) & 3), 8:16]
        found = jnp.concatenate([pack[top : top + 1], pack[top + 1 : top + 2]], axis=1)
        return jnp.where(gz == (3 if up else 0), 0.0, found)

    def edge(up, top):
        y = lane & 7
        beside = jnp.where(y == 0, rows(1, up, top), 0.0)
        return jnp.where(y == 7, rows(7, up, top), beside)

    inner = jnp.concatenate(
        [rows(0, True, 0), rows(0, False, 2), rows(0, True, 4), rows(0, False, 6)], axis=0
    )
    inner = exact(inner, lanes(4, (0, 127, 1, 126)), (0,)).reshape(4, 8, 8, 128)
    edges = jnp.concatenate([edge(True, 0), edge(False, 2)], axis=0)
    ghosts[:, :, 0:8] = inner
    ghosts[:, :, 8:16] = exact(edges, lanes(2, (0, 127)), (0,)).reshape(4, 8, 8, 128)

    even = (gx & 1) == 0
    row = lax.broadcasted_iota(jnp.int32, (1, 8, 128), 1)

    def slab(x, near):
        beside = jnp.where(
            row == 0, yhi[:, near, 0:1], jnp.where(row == 7, ylo[:, near, 1:2], 0.0)
        )
        return [state[:, x], state[:, x + 1], beside, inner[:, near]]

    for i, (high, low) in enumerate(zip(slab(6, 7), slab(0, 0))):
        first[:, i] = jnp.where(even, high, low)
        second[:, i] = jnp.where(even, low, high)


def spread_kernel(parts, cell, dest, elem, weight, before, new_state, body_force):
    match, hot_lane = element_keys(dest[...], elem[...])
    found = pick(parts[...].reshape(256, 128), hot_lane).reshape(32, 8, ROWS)
    pairs = jnp.sum(jnp.where(match, found, 0.0), axis=0)
    column, hot_z = cell_keys(cell[...])
    each = [(pairs[2 * c : 2 * c + 1] + pairs[2 * c + 1 : 2 * c + 2]) * weight[...] for c in range(3)]
    spread = jnp.concatenate([jnp.where(column, each[c], 0.0) for c in range(3)], axis=0)
    body = put(spread, hot_z).reshape(3, 8, 8, 128)
    body_force[...] = body
    new_state[0:3] = before[0:3] + DT_STEP * body
    new_state[3] = before[3]


def stencil_kernel(state, ylo, yhi, ghosts, first, second, before, grid):
    gz = lax.axis_index("gz")
    fill(grid, state, ylo, yhi, ghosts, first, second)
    level = lax.broadcasted_iota(jnp.int32, (1, 1, 256), 2)
    outside = ((level >= 128) & (level < 192) & (gz == 3)) | ((level >= 192) & (gz == 0))

    def around(values):
        return (
            (pltpu.roll(values, 15, 1), pltpu.roll(values, 1, 1)),
            (pltpu.roll(values, 255, 2), pltpu.roll(values, 1, 2)),
        )

    fields = [grid[c] for c in range(4)]
    sides = []
    diffs = []
    for c in range(4):
        middle = fields[c][1:11]
        near = ((fields[c][2:12], fields[c][0:10]),) + around(middle)
        sides.append(near)
        diffs.append([upper - lower for upper, lower in near])
    strain = 0.5 * (
        diffs[0][0] * diffs[0][0] + diffs[1][1] * diffs[1][1] + diffs[2][2] * diffs[2][2]
    )
    for i, j in ((0, 1), (0, 2), (1, 2)):
        paired = diffs[i][j] + diffs[j][i]
        strain = strain + 0.25 * paired * paired
    eddy = jnp.where(outside, 0.0, SMAG_COEF * jnp.sqrt(strain))

    def inner(values):
        return values[:, 0:8, 0:128]

    centre = inner(eddy[1:9])
    near = ((eddy[2:10], eddy[0:8]),) + around(eddy[1:9])
    faces = [[0.5 * (centre + inner(side)) for side in pair] for pair in near]
    wind = [0.5 * inner(fields[c][2:10]) for c in range(3)]
    for c in range(4):
        middle = inner(fields[c][2:10])
        ratio = 1.0 if c < 3 else 1.0 / PRANDTL
        change = 0.0
        for j in range(3):
            upper, lower = [inner(side[1:9]) for side in sides[c][j]]
            change = change + (BASE_COEF + ratio * faces[j][0]) * (upper - middle)
            change = change - (BASE_COEF + ratio * faces[j][1]) * (middle - lower)
            change = change - wind[j] * (upper - lower)
        before[c] = middle + DT_STEP * change


def shift(up, down, axis):
    count = lax.axis_size(axis)
    forward = [(i, (i + 1) % count) for i in range(count)]
    backward = [(target, source) for source, target in forward]
    return lax.ppermute(up, axis, forward), lax.ppermute(down, axis, backward)


def swap(slab, axis, odd):
    count = lax.axis_size(axis)
    return lax.ppermute(
        slab, axis, [(i, (i + 1 if i % 2 == odd else i - 1) % count) for i in range(count)]
    )


def exchange(blocks, axes):
    return lax.all_to_all(blocks, axes, split_axis=0, concat_axis=0, tiled=True)


def body(state, sample_cell, sample_dest, sample_weight, sample_elem, element_motion, element_coef):
    cell = sample_cell.reshape(1, ROWS)
    dest = sample_dest.reshape(1, ROWS)
    elem = sample_elem.reshape(1, ROWS)
    weight = sample_weight.reshape(1, ROWS)

    coef = element_coef.reshape(1, 128)
    rows = pltpu.VMEM((1, ROWS), jnp.int32)
    held = (
        pltpu.VMEM((4, 8, 8, 128), jnp.float32),
        rows,
        rows,
        rows,
        pltpu.VMEM((1, ROWS), jnp.float32),
        pltpu.VMEM((3, 128), jnp.float32),
        pltpu.VMEM((1, 128), jnp.float32),
        pltpu.SemaphoreType.DMA((7,)),
    )
    side = f32(4, 8, 2, 128)
    partial, own, yup, ydown = call(
        sample_kernel,
        (f32(32, 16, 128), f32(8, 128), side, side),
        held,
        7,
        pltpu.HBM,
        60 * 1024 * 1024,
    )(state, cell, dest, elem, weight, element_motion, coef)
    parts = exchange(partial, PLANE)
    ylo, yhi = shift(yup, ydown, "gy")
    parts, ylo, yhi = lax.optimization_barrier((parts, ylo, yhi))

    totals = call(total_kernel, f32(16, 8, 128), count=2)(parts, own)
    totals = exchange(totals, "gx")
    slab = f32(4, 4, 8, 128)
    first, second, ghosts = call(faces_kernel, (slab, slab, f32(4, 8, 16, 128)), count=4)(
        parts, state, ylo, yhi
    )
    first, second = swap(first, "gx", 0), swap(second, "gx", 1)
    totals, first, second = lax.optimization_barrier((totals, first, second))

    forces = call(force_kernel, f32(32, 8, 128), count=1)(totals)
    forces = exchange(forces, PLANE)
    grid = pltpu.VMEM((4, 12, 16, 256), jnp.float32)
    before = call(stencil_kernel, f32(4, 8, 8, 128), (grid,), 6)(
        state, ylo, yhi, ghosts, first, second
    )
    return call(spread_kernel, (f32(4, 8, 8, 128), f32(3, 8, 8, 128)), count=6)(
        forces, cell, dest, elem, weight, before
    )


def solution(mesh):
    return jax.shard_map(
        body,
        mesh=mesh,
        in_specs=(
            P(None, "gx", "gy", "gz"),
            P(("gx", "gy", "gz")),
            P(("gx", "gy", "gz"), None),
            P(("gx", "gy", "gz")),
            P(("gx", "gy", "gz")),
            P(None, ("gx", "gz")),
            P(("gx", "gz")),
        ),
        out_specs=(P(None, "gx", "gy", "gz"), P(None, "gx", "gy", "gz")),
        check_vma=False,
    )
```

```python
import jax
import jax.numpy as jnp
from jax import lax
from jax.experimental import pallas as pl
from jax.experimental.pallas import tpu as pltpu
from jax.sharding import PartitionSpec as P

DT_STEP = 0.4
BASE_COEF = 0.02
PRANDTL = 0.7
SMAG_COEF = 0.04

ROWS = 1024
PLANE = ("gy", "gz")


def call(kernel, outs, scratch=(), count=1, space=pltpu.VMEM, limit=24 * 1024 * 1024):
    return pl.pallas_call(
        kernel,
        out_shape=outs,
        in_specs=[pl.BlockSpec(memory_space=space)] * count,
        out_specs=jax.tree.map(lambda _: pl.BlockSpec(memory_space=pltpu.VMEM), outs),
        scratch_shapes=scratch,
        compiler_params=pltpu.CompilerParams(vmem_limit_bytes=limit),
        cost_estimate=pl.CostEstimate(
            flops=2_000_000, bytes_accessed=1_000_000, transcendentals=0
        ),
    )


def f32(*shape):
    return jax.ShapeDtypeStruct(shape, jnp.float32)


def halves(values):
    high = values.astype(jnp.bfloat16)
    return high, (values - high.astype(jnp.float32)).astype(jnp.bfloat16)


def onehot(index, size):
    wanted = lax.broadcasted_iota(jnp.int32, (size, ROWS), 0)
    return jnp.where(wanted == index, 1.0, 0.0).astype(jnp.bfloat16)


def pick(table, hot):
    both = jnp.concatenate(halves(table), axis=1)
    return jnp.dot(both, jnp.concatenate([hot, hot], axis=0), preferred_element_type=jnp.float32)


def put(values, hot):
    high, low = halves(values)
    dims = (((1,), (1,)), ((), ()))
    total = lax.dot_general(high, hot, dims, preferred_element_type=jnp.float32)
    return total + lax.dot_general(low, hot, dims, preferred_element_type=jnp.float32)


def cell_keys(cell):
    column = lax.broadcasted_iota(jnp.int32, (64, ROWS), 0) == (cell >> 7)
    return column, onehot(cell & 127, 128)


def element_keys(dest, elem):
    tile = (elem >> 4) * 4 + (dest & 3)
    along = dest >> 2
    number = tile * 2 + (along >> 3)
    shape = (32, 8, ROWS)
    row = lax.broadcasted_iota(jnp.int32, shape, 0) * 2 + (
        lax.broadcasted_iota(jnp.int32, shape, 1) & 1
    )
    return row == number[None], onehot((along & 7) * 16 + (elem & 15), 128)


def own_part(motion, coef):
    gx, gy = lax.axis_index("gx"), lax.axis_index("gy")
    row = lax.broadcasted_iota(jnp.int32, (8, 128), 0)
    lane = lax.broadcasted_iota(jnp.int32, (8, 128), 1)
    level = row >> 1
    held = jnp.where(
        level == 0,
        motion[0:1, :],
        jnp.where(level == 1, motion[1:2, :], jnp.where(level == 2, motion[2:3, :], coef[...])),
    )
    moved = pltpu.roll(held, ((gx & 7) * 16 - gy * 16 + 128) & 127, 1)
    mine = ((lane >> 4) == (gx & 7)) & ((row & 1) == (gx >> 3))
    return jnp.where(mine, moved, 0.0)


def lanes(count, places):
    row = lax.broadcasted_iota(jnp.int32, (count, 128), 0)
    lane = lax.broadcasted_iota(jnp.int32, (count, 128), 1)
    hot = (row == 0) & (lane == places[0])
    for i, place in enumerate(places[1:]):
        hot = hot | ((row == i + 1) & (lane == place))
    return jnp.where(hot, 1.0, 0.0)


def thirds(values):
    high, rest = halves(values)
    low = values - high.astype(jnp.float32) - rest.astype(jnp.float32)
    return high, rest, low.astype(jnp.bfloat16)


def take_lanes(places, rows):
    hot = lanes(8, places).astype(jnp.bfloat16)
    dims = (((1,), (1,)), ((), ()))
    parts = [
        lax.dot_general(hot, part, dims, preferred_element_type=jnp.float32)
        for part in thirds(rows)
    ]
    return parts[0] + parts[1] + parts[2]


def give_lanes(rows, places):
    hot = lanes(len(places), places)
    return lax.dot_general(
        jnp.concatenate(thirds(rows), axis=0),
        jnp.concatenate([hot, hot, hot], axis=0).astype(jnp.bfloat16),
        (((0,), (0,)), ((), ())),
        preferred_element_type=jnp.float32,
    )


def sample_kernel(
    state_in,
    cell_in,
    dest_in,
    elem_in,
    weight_in,
    motion_in,
    coef_in,
    out,
    own,
    first,
    second,
    *scratch,
):
    held, sems = scratch[:7], scratch[7]
    sources = (state_in, cell_in, dest_in, elem_in, weight_in, motion_in, coef_in)
    copies = [
        pltpu.make_async_copy(source, target, sems.at[i])
        for i, (source, target) in enumerate(zip(sources, held))
    ]
    for copy in copies:
        copy.start()
    for copy in copies:
        copy.wait()
    state, cell, dest, elem, weight, motion, coef = held
    own[...] = own_part(motion, coef)
    even = (lax.axis_index("gx") & 1) == 0
    first[...] = jnp.where(even, state[:, 6:8], state[:, 0:2])
    second[...] = jnp.where(even, state[:, 0:2], state[:, 6:8])
    column, hot_z = cell_keys(cell[...])
    found = pick(state[0:3].reshape(192, 128), hot_z).reshape(3, 64, ROWS)
    sampled = [
        jnp.sum(jnp.where(column, found[c], 0.0), axis=0, keepdims=True) * weight[...]
        for c in range(3)
    ]
    row = lax.broadcasted_iota(jnp.int32, (8, ROWS), 0) >> 1
    pattern = jnp.where(
        row == 0, sampled[0], jnp.where(row == 1, sampled[1], jnp.where(row == 2, sampled[2], 0.0))
    )
    match, hot_lane = element_keys(dest[...], elem[...])
    spread = jnp.where(match, pattern[None], 0.0).reshape(256, ROWS)
    out[...] = put(spread, hot_lane).reshape(32, 8, 128)


def total_kernel(parts, own, out):
    total = jnp.sum(parts[...], axis=0) + own[...]
    out[...] = jnp.broadcast_to(total[None], (16, 8, 128))


def force_kernel(parts, packs, out):
    total = jnp.sum(parts[...], axis=0)
    row = lax.broadcasted_iota(jnp.int32, (8, 128), 0)

    def by_parity(values):
        values = values + pltpu.roll(values, 4, 0)
        return values + pltpu.roll(values, 2, 0)

    speed = jnp.sqrt(by_parity(jnp.where(row < 6, total * total, 0.0)))
    coef = by_parity(jnp.where(row < 6, 0.0, total))
    force = jnp.where(row < 6, -coef * speed * total, 0.0)
    out[:, 0:8] = jnp.broadcast_to(force[None], (32, 8, 128))
    above = (lax.axis_index("gz") + 1) & 3
    for level in range(4):
        pack = jnp.where(above == level, packs[1], packs[0])
        for across in range(8):
            out[4 * across + level, 8:16] = pack


def beside(first, second):
    even = (lax.axis_index("gx") & 1) == 0
    first, second = first[...], second[...]
    return jnp.where(even, second, first), jnp.where(even, first, second)


def faces_kernel(state, first, second, yup, ydown, packs):
    xlo, xhi = beside(first, second)
    wide = jnp.concatenate([xlo, state[...], xhi], axis=1)
    yup[...] = wide[:, 1:11, 6:8]
    ydown[...] = wide[:, 1:11, 0:2]
    ends = take_lanes((0, 1, 127, 126), wide.reshape(384, 128))
    blank = jnp.zeros((2, 128), jnp.float32)
    for side in range(2):
        pieces = [
            ends[2 * side + i : 2 * side + i + 1, 128 * j : 128 * j + 128]
            for i in range(2)
            for j in range(3)
        ]
        packs[side] = jnp.concatenate(pieces + [blank], axis=0)


def fill(grid, parts, state, ylo, yhi, first, second):
    gy, gz = lax.axis_index("gy"), lax.axis_index("gz")
    xlo, xhi = beside(first, second)
    grid[:, 0:2, 0:8, 0:128] = xlo
    grid[:, 2:10, 0:8, 0:128] = state[...]
    grid[:, 10:12, 0:8, 0:128] = xhi
    grid[:, 1:11, 8:10, 0:128] = yhi[...]
    grid[:, 1:11, 14:16, 0:128] = ylo[...]

    def rows(across, up, far):
        pack = parts[((gy + across) & 7) * 4 + ((gz + (1 if up else 3)) & 3), 8:16]
        found = jnp.concatenate([pack[i : i + 1] for i in range(3 * far, 3 * far + 3)], axis=1)
        return jnp.where(gz == (3 if up else 0), 0.0, found)

    y = lax.broadcasted_iota(jnp.int32, (1, 384), 1) & 7

    def edge(up):
        over = jnp.where(y == 0, rows(1, up, 0), 0.0)
        return jnp.where(y == 7, rows(7, up, 0), over)

    inner = [rows(0, True, 0), rows(0, False, 0), rows(0, True, 1), rows(0, False, 1)]
    inner = give_lanes(jnp.concatenate(inner, axis=0), (0, 127, 1, 126))
    edges = give_lanes(jnp.concatenate([edge(True), edge(False)], axis=0), (0, 127))
    grid[:, :, 0:8, 128:256] = inner.reshape(4, 12, 8, 128)
    grid[:, :, 8:16, 128:256] = edges.reshape(4, 12, 8, 128)


def final_kernel(
    parts, cell, dest, elem, weight, state, ylo, yhi, first, second, *results
):
    new_state, body_force, grid = results
    match, hot_lane = element_keys(dest[...], elem[...])
    found = pick(parts[:, 0:8].reshape(256, 128), hot_lane).reshape(32, 8, ROWS)
    pairs = jnp.sum(jnp.where(match, found, 0.0), axis=0)
    column, hot_z = cell_keys(cell[...])
    each = [(pairs[2 * c : 2 * c + 1] + pairs[2 * c + 1 : 2 * c + 2]) * weight[...] for c in range(3)]
    spread = jnp.concatenate([jnp.where(column, each[c], 0.0) for c in range(3)], axis=0)
    body = put(spread, hot_z).reshape(3, 8, 8, 128)
    body_force[...] = body

    gz = lax.axis_index("gz")
    fill(grid, parts, state, ylo, yhi, first, second)
    level = lax.broadcasted_iota(jnp.int32, (1, 1, 256), 2)
    outside = ((level >= 128) & (level < 192) & (gz == 3)) | ((level >= 192) & (gz == 0))

    def around(values):
        return (
            (pltpu.roll(values, 15, 1), pltpu.roll(values, 1, 1)),
            (pltpu.roll(values, 255, 2), pltpu.roll(values, 1, 2)),
        )

    fields = [grid[c] for c in range(4)]
    sides = []
    diffs = []
    for c in range(4):
        middle = fields[c][1:11]
        near = ((fields[c][2:12], fields[c][0:10]),) + around(middle)
        sides.append(near)
        diffs.append([upper - lower for upper, lower in near])
    strain = 0.5 * (
        diffs[0][0] * diffs[0][0] + diffs[1][1] * diffs[1][1] + diffs[2][2] * diffs[2][2]
    )
    for i, j in ((0, 1), (0, 2), (1, 2)):
        paired = diffs[i][j] + diffs[j][i]
        strain = strain + 0.25 * paired * paired
    eddy = jnp.where(outside, 0.0, SMAG_COEF * jnp.sqrt(strain))

    def inner(values):
        return values[:, 0:8, 0:128]

    centre = inner(eddy[1:9])
    near = ((eddy[2:10], eddy[0:8]),) + around(eddy[1:9])
    faces = [[0.5 * (centre + inner(side)) for side in pair] for pair in near]
    wind = [0.5 * inner(fields[c][2:10]) for c in range(3)]
    for c in range(4):
        middle = inner(fields[c][2:10])
        ratio = 1.0 if c < 3 else 1.0 / PRANDTL
        change = 0.0
        for j in range(3):
            upper, lower = [inner(side[1:9]) for side in sides[c][j]]
            change = change + (BASE_COEF + ratio * faces[j][0]) * (upper - middle)
            change = change - (BASE_COEF + ratio * faces[j][1]) * (middle - lower)
            change = change - wind[j] * (upper - lower)
        if c < 3:
            change = change + body[c]
        new_state[c] = middle + DT_STEP * change


def shift(up, down, axis):
    count = lax.axis_size(axis)
    forward = [(i, (i + 1) % count) for i in range(count)]
    backward = [(target, source) for source, target in forward]
    return lax.ppermute(up, axis, forward), lax.ppermute(down, axis, backward)


def swap(slab, axis, odd):
    count = lax.axis_size(axis)
    return lax.ppermute(
        slab, axis, [(i, (i + 1 if i % 2 == odd else i - 1) % count) for i in range(count)]
    )


def exchange(blocks, axes):
    return lax.all_to_all(blocks, axes, split_axis=0, concat_axis=0, tiled=True)


def body(state, sample_cell, sample_dest, sample_weight, sample_elem, element_motion, element_coef):
    cell = sample_cell.reshape(1, ROWS)
    dest = sample_dest.reshape(1, ROWS)
    elem = sample_elem.reshape(1, ROWS)
    weight = sample_weight.reshape(1, ROWS)

    coef = element_coef.reshape(1, 128)
    rows = pltpu.VMEM((1, ROWS), jnp.int32)
    held = (
        pltpu.VMEM((4, 8, 8, 128), jnp.float32),
        rows,
        rows,
        rows,
        pltpu.VMEM((1, ROWS), jnp.float32),
        pltpu.VMEM((3, 128), jnp.float32),
        pltpu.VMEM((1, 128), jnp.float32),
        pltpu.SemaphoreType.DMA((7,)),
    )
    slab = f32(4, 2, 8, 128)
    parts, own, first, second = call(
        sample_kernel,
        (f32(32, 8, 128), f32(8, 128), slab, slab),
        held,
        7,
        pltpu.HBM,
        60 * 1024 * 1024,
    )(state, cell, dest, elem, weight, element_motion, coef)
    parts = exchange(parts, PLANE)
    first = swap(first, "gx", 0)
    parts, first = lax.optimization_barrier((parts, first))

    totals = call(total_kernel, f32(16, 8, 128), count=2)(parts, own)
    totals, second = lax.optimization_barrier((totals, second))
    totals = exchange(totals, "gx")
    second = swap(second, "gx", 1)
    side = f32(4, 10, 2, 128)
    yup, ydown, packs = call(faces_kernel, (side, side, f32(2, 8, 128)), count=3)(
        state, first, second
    )

    forces = call(force_kernel, f32(32, 16, 128), count=2)(totals, packs)
    forces, yup, ydown = lax.optimization_barrier((forces, yup, ydown))
    forces = exchange(forces, PLANE)
    ylo, yhi = shift(yup, ydown, "gy")
    grid = pltpu.VMEM((4, 12, 16, 256), jnp.float32)
    return call(final_kernel, (f32(4, 8, 8, 128), f32(3, 8, 8, 128)), (grid,), 10)(
        forces, cell, dest, elem, weight, state, ylo, yhi, first, second
    )


def solution(mesh):
    return jax.shard_map(
        body,
        mesh=mesh,
        in_specs=(
            P(None, "gx", "gy", "gz"),
            P(("gx", "gy", "gz")),
            P(("gx", "gy", "gz"), None),
            P(("gx", "gy", "gz")),
            P(("gx", "gy", "gz")),
            P(None, ("gx", "gz")),
            P(("gx", "gz")),
        ),
        out_specs=(P(None, "gx", "gy", "gz"), P(None, "gx", "gy", "gz")),
        check_vma=False,
    )
```

```python
import jax
import jax.numpy as jnp
from jax import lax
from jax.experimental import pallas as pl
from jax.experimental.pallas import tpu as pltpu
from jax.sharding import PartitionSpec as P

DT_STEP = 0.4
BASE_COEF = 0.02
PRANDTL = 0.7
SMAG_COEF = 0.04

ROWS = 1024
PLANE = ("gy", "gz")


def call(kernel, outs, scratch=(), count=1, space=pltpu.VMEM, limit=24 * 1024 * 1024):
    return pl.pallas_call(
        kernel,
        out_shape=outs,
        in_specs=[pl.BlockSpec(memory_space=space)] * count,
        out_specs=jax.tree.map(lambda _: pl.BlockSpec(memory_space=pltpu.VMEM), outs),
        scratch_shapes=scratch,
        compiler_params=pltpu.CompilerParams(vmem_limit_bytes=limit),
        cost_estimate=pl.CostEstimate(
            flops=2_000_000, bytes_accessed=1_000_000, transcendentals=0
        ),
    )


def f32(*shape):
    return jax.ShapeDtypeStruct(shape, jnp.float32)


def halves(values):
    high = values.astype(jnp.bfloat16)
    return high, (values - high.astype(jnp.float32)).astype(jnp.bfloat16)


def onehot(index, size):
    wanted = lax.broadcasted_iota(jnp.int32, (size, ROWS), 0)
    return jnp.where(wanted == index, 1.0, 0.0).astype(jnp.bfloat16)


def pick(table, hot):
    both = jnp.concatenate(halves(table), axis=1)
    return jnp.dot(both, jnp.concatenate([hot, hot], axis=0), preferred_element_type=jnp.float32)


def put(values, hot):
    high, low = halves(values)
    dims = (((1,), (1,)), ((), ()))
    total = lax.dot_general(high, hot, dims, preferred_element_type=jnp.float32)
    return total + lax.dot_general(low, hot, dims, preferred_element_type=jnp.float32)


def cell_keys(cell):
    column = lax.broadcasted_iota(jnp.int32, (64, ROWS), 0) == (cell >> 7)
    return column, onehot(cell & 127, 128)


def element_keys(dest, elem):
    tile = (elem >> 4) * 4 + (dest & 3)
    along = dest >> 2
    number = tile * 2 + (along >> 3)
    shape = (32, 8, ROWS)
    row = lax.broadcasted_iota(jnp.int32, shape, 0) * 2 + (
        lax.broadcasted_iota(jnp.int32, shape, 1) & 1
    )
    return row == number[None], onehot((along & 7) * 16 + (elem & 15), 128)


def own_part(motion, coef):
    gx, gy = lax.axis_index("gx"), lax.axis_index("gy")
    row = lax.broadcasted_iota(jnp.int32, (8, 128), 0)
    lane = lax.broadcasted_iota(jnp.int32, (8, 128), 1)
    level = row >> 1
    held = jnp.where(
        level == 0,
        motion[0:1, :],
        jnp.where(level == 1, motion[1:2, :], jnp.where(level == 2, motion[2:3, :], coef[...])),
    )
    moved = pltpu.roll(held, ((gx & 7) * 16 - gy * 16 + 128) & 127, 1)
    mine = ((lane >> 4) == (gx & 7)) & ((row & 1) == (gx >> 3))
    return jnp.where(mine, moved, 0.0)


def lanes(count, places):
    row = lax.broadcasted_iota(jnp.int32, (count, 128), 0)
    lane = lax.broadcasted_iota(jnp.int32, (count, 128), 1)
    hot = (row == 0) & (lane == places[0])
    for i, place in enumerate(places[1:]):
        hot = hot | ((row == i + 1) & (lane == place))
    return jnp.where(hot, 1.0, 0.0)


def thirds(values):
    high, rest = halves(values)
    low = values - high.astype(jnp.float32) - rest.astype(jnp.float32)
    return high, rest, low.astype(jnp.bfloat16)


def take_lanes(places, rows):
    hot = lanes(8, places).astype(jnp.bfloat16)
    dims = (((1,), (1,)), ((), ()))
    parts = [
        lax.dot_general(hot, part, dims, preferred_element_type=jnp.float32)
        for part in thirds(rows)
    ]
    return parts[0] + parts[1] + parts[2]


def give_lanes(rows, places):
    hot = lanes(len(places), places)
    return lax.dot_general(
        jnp.concatenate(thirds(rows), axis=0),
        jnp.concatenate([hot, hot, hot], axis=0).astype(jnp.bfloat16),
        (((0,), (0,)), ((), ())),
        preferred_element_type=jnp.float32,
    )


def sample_kernel(
    state_in,
    cell_in,
    dest_in,
    elem_in,
    weight_in,
    motion_in,
    coef_in,
    out,
    own,
    yup,
    ydown,
    *scratch,
):
    held, sems = scratch[:7], scratch[7]
    sources = (state_in, cell_in, dest_in, elem_in, weight_in, motion_in, coef_in)
    copies = [
        pltpu.make_async_copy(source, target, sems.at[i])
        for i, (source, target) in enumerate(zip(sources, held))
    ]
    for copy in copies:
        copy.start()
    for copy in copies:
        copy.wait()
    state, cell, dest, elem, weight, motion, coef = held
    own[...] = own_part(motion, coef)
    yup[...] = state[:, :, 6:8]
    ydown[...] = state[:, :, 0:2]
    ends = take_lanes((0, 127, 1, 126), state[...].reshape(256, 128))
    pack = [ends[i : i + 1, 128 * j : 128 * j + 128] for i in range(4) for j in range(2)]
    out[:, 8:16] = jnp.broadcast_to(jnp.concatenate(pack, axis=0)[None], (32, 8, 128))
    column, hot_z = cell_keys(cell[...])
    found = pick(state[0:3].reshape(192, 128), hot_z).reshape(3, 64, ROWS)
    sampled = [
        jnp.sum(jnp.where(column, found[c], 0.0), axis=0, keepdims=True) * weight[...]
        for c in range(3)
    ]
    row = lax.broadcasted_iota(jnp.int32, (8, ROWS), 0) >> 1
    pattern = jnp.where(
        row == 0, sampled[0], jnp.where(row == 1, sampled[1], jnp.where(row == 2, sampled[2], 0.0))
    )
    match, hot_lane = element_keys(dest[...], elem[...])
    spread = jnp.where(match, pattern[None], 0.0).reshape(256, ROWS)
    out[:, 0:8] = put(spread, hot_lane).reshape(32, 8, 128)


def total_kernel(parts, own, out):
    total = jnp.sum(parts[:, 0:8], axis=0) + own[...]
    out[...] = jnp.broadcast_to(total[None], (16, 8, 128))


def force_kernel(parts, out):
    total = jnp.sum(parts[...], axis=0)
    row = lax.broadcasted_iota(jnp.int32, (8, 128), 0)

    def by_parity(values):
        values = values + pltpu.roll(values, 4, 0)
        return values + pltpu.roll(values, 2, 0)

    speed = jnp.sqrt(by_parity(jnp.where(row < 6, total * total, 0.0)))
    coef = by_parity(jnp.where(row < 6, 0.0, total))
    force = jnp.where(row < 6, -coef * speed * total, 0.0)
    out[...] = jnp.broadcast_to(force[None], (32, 8, 128))


def fill(grid, state, ylo, yhi, ghosts, first, second):
    grid[:, 2:10, 0:8, 0:128] = state[...]
    grid[:, 2:10, 8:10, 0:128] = yhi[...]
    grid[:, 2:10, 14:16, 0:128] = ylo[...]
    grid[:, 2:10, :, 128:256] = ghosts[...]
    even = (lax.axis_index("gx") & 1) == 0
    row = lax.broadcasted_iota(jnp.int32, (8, 128), 0)
    column = lax.broadcasted_iota(jnp.int32, (8, 128), 1)
    outer = (column == 0) | (column == 127)
    for plane, near, slab in (
        (0, 1, jnp.where(even, second[...], first[...])),
        (10, 10, jnp.where(even, first[...], second[...])),
    ):
        for c in range(4):
            grid[c, plane, 0:8, 0:128] = slab[2 * c]
            grid[c, plane + 1, 0:8, 0:128] = slab[2 * c + 1]
            over, under = slab[8, 2 * c : 2 * c + 1], slab[8, 2 * c + 1 : 2 * c + 2]
            grid[c, near, 8:16, 0:128] = jnp.where(row == 0, over, jnp.where(row == 7, under, 0.0))
            ends = slab[9] if c == 0 else pltpu.roll(slab[9], 128 - 2 * c, 1)
            grid[c, near, 0:8, 128:256] = jnp.where(outer, ends, 0.0)


def faces_kernel(parts, state, ylo, yhi, first, second, ghosts):
    gx, gy, gz = [lax.axis_index(axis) for axis in ("gx", "gy", "gz")]
    lane = lax.broadcasted_iota(jnp.int32, (1, 256), 1)

    def rows(across, up, top):
        pack = parts[((gy + across) & 7) * 4 + ((gz + (1 if up else 3)) & 3), 8:16]
        found = jnp.concatenate([pack[top : top + 1], pack[top + 1 : top + 2]], axis=1)
        return jnp.where(gz == (3 if up else 0), 0.0, found)

    def edge(up, top):
        y = lane & 7
        beside = jnp.where(y == 0, rows(1, up, top), 0.0)
        return jnp.where(y == 7, rows(7, up, top), beside)

    inner = jnp.concatenate(
        [rows(0, True, 0), rows(0, False, 2), rows(0, True, 4), rows(0, False, 6)], axis=0
    )
    inner = give_lanes(inner, (0, 127, 1, 126)).reshape(4, 8, 8, 128)
    edges = jnp.concatenate([edge(True, 0), edge(False, 2)], axis=0)
    ghosts[:, :, 0:8] = inner
    ghosts[:, :, 8:16] = give_lanes(edges, (0, 127)).reshape(4, 8, 8, 128)

    even = (gx & 1) == 0
    column = lax.broadcasted_iota(jnp.int32, (8, 128), 1)
    outer = (column == 0) | (column == 127)

    def slab(x, near):
        tiles = [state[c, x + i] for c in range(4) for i in range(2)]
        across = [part[c, near, i : i + 1] for c in range(4) for part, i in ((yhi, 0), (ylo, 1))]
        ends = [jnp.where(outer, inner[c, near], 0.0) for c in range(4)]
        ends = [ends[0]] + [pltpu.roll(ends[c], 2 * c, 1) for c in range(1, 4)]
        return tiles + [jnp.concatenate(across, axis=0), ends[0] + ends[1] + ends[2] + ends[3]]

    for i, (high, low) in enumerate(zip(slab(6, 7), slab(0, 0))):
        first[i] = jnp.where(even, high, low)
        second[i] = jnp.where(even, low, high)


def final_kernel(
    parts, cell, dest, elem, weight, state, ylo, yhi, ghosts, first, second, *results
):
    new_state, body_force, grid = results
    match, hot_lane = element_keys(dest[...], elem[...])
    found = pick(parts[...].reshape(256, 128), hot_lane).reshape(32, 8, ROWS)
    pairs = jnp.sum(jnp.where(match, found, 0.0), axis=0)
    column, hot_z = cell_keys(cell[...])
    each = [(pairs[2 * c : 2 * c + 1] + pairs[2 * c + 1 : 2 * c + 2]) * weight[...] for c in range(3)]
    spread = jnp.concatenate([jnp.where(column, each[c], 0.0) for c in range(3)], axis=0)
    body = put(spread, hot_z).reshape(3, 8, 8, 128)
    body_force[...] = body

    gz = lax.axis_index("gz")
    fill(grid, state, ylo, yhi, ghosts, first, second)
    level = lax.broadcasted_iota(jnp.int32, (1, 1, 256), 2)
    outside = ((level >= 128) & (level < 192) & (gz == 3)) | ((level >= 192) & (gz == 0))

    def around(values):
        return (
            (pltpu.roll(values, 15, 1), pltpu.roll(values, 1, 1)),
            (pltpu.roll(values, 255, 2), pltpu.roll(values, 1, 2)),
        )

    fields = [grid[c] for c in range(4)]
    sides = []
    diffs = []
    for c in range(4):
        middle = fields[c][1:11]
        near = ((fields[c][2:12], fields[c][0:10]),) + around(middle)
        sides.append(near)
        diffs.append([upper - lower for upper, lower in near])
    strain = 0.5 * (
        diffs[0][0] * diffs[0][0] + diffs[1][1] * diffs[1][1] + diffs[2][2] * diffs[2][2]
    )
    for i, j in ((0, 1), (0, 2), (1, 2)):
        paired = diffs[i][j] + diffs[j][i]
        strain = strain + 0.25 * paired * paired
    eddy = jnp.where(outside, 0.0, SMAG_COEF * jnp.sqrt(strain))

    def inner(values):
        return values[:, 0:8, 0:128]

    centre = inner(eddy[1:9])
    near = ((eddy[2:10], eddy[0:8]),) + around(eddy[1:9])
    faces = [[0.5 * (centre + inner(side)) for side in pair] for pair in near]
    wind = [0.5 * inner(fields[c][2:10]) for c in range(3)]
    for c in range(4):
        middle = inner(fields[c][2:10])
        ratio = 1.0 if c < 3 else 1.0 / PRANDTL
        change = 0.0
        for j in range(3):
            upper, lower = [inner(side[1:9]) for side in sides[c][j]]
            change = change + (BASE_COEF + ratio * faces[j][0]) * (upper - middle)
            change = change - (BASE_COEF + ratio * faces[j][1]) * (middle - lower)
            change = change - wind[j] * (upper - lower)
        if c < 3:
            change = change + body[c]
        new_state[c] = middle + DT_STEP * change


def shift(up, down, axis):
    count = lax.axis_size(axis)
    forward = [(i, (i + 1) % count) for i in range(count)]
    backward = [(target, source) for source, target in forward]
    return lax.ppermute(up, axis, forward), lax.ppermute(down, axis, backward)


def swap(slab, axis, odd):
    count = lax.axis_size(axis)
    return lax.ppermute(
        slab, axis, [(i, (i + 1 if i % 2 == odd else i - 1) % count) for i in range(count)]
    )


def exchange(blocks, axes):
    return lax.all_to_all(blocks, axes, split_axis=0, concat_axis=0, tiled=True)


def body(state, sample_cell, sample_dest, sample_weight, sample_elem, element_motion, element_coef):
    cell = sample_cell.reshape(1, ROWS)
    dest = sample_dest.reshape(1, ROWS)
    elem = sample_elem.reshape(1, ROWS)
    weight = sample_weight.reshape(1, ROWS)

    coef = element_coef.reshape(1, 128)
    rows = pltpu.VMEM((1, ROWS), jnp.int32)
    held = (
        pltpu.VMEM((4, 8, 8, 128), jnp.float32),
        rows,
        rows,
        rows,
        pltpu.VMEM((1, ROWS), jnp.float32),
        pltpu.VMEM((3, 128), jnp.float32),
        pltpu.VMEM((1, 128), jnp.float32),
        pltpu.SemaphoreType.DMA((7,)),
    )
    side = f32(4, 8, 2, 128)
    partial, own, yup, ydown = call(
        sample_kernel,
        (f32(32, 16, 128), f32(8, 128), side, side),
        held,
        7,
        pltpu.HBM,
        60 * 1024 * 1024,
    )(state, cell, dest, elem, weight, element_motion, coef)
    parts = exchange(partial, PLANE)
    ylo, yhi = shift(yup, ydown, "gy")
    parts, ylo, yhi = lax.optimization_barrier((parts, ylo, yhi))

    totals = call(total_kernel, f32(16, 8, 128), count=2)(parts, own)
    totals = exchange(totals, "gx")
    slab = f32(10, 8, 128)
    first, second, ghosts = call(faces_kernel, (slab, slab, f32(4, 8, 16, 128)), count=4)(
        parts, state, ylo, yhi
    )
    first, second = swap(first, "gx", 0), swap(second, "gx", 1)
    totals, first, second = lax.optimization_barrier((totals, first, second))

    forces = call(force_kernel, f32(32, 8, 128), count=1)(totals)
    forces = exchange(forces, PLANE)
    grid = pltpu.VMEM((4, 12, 16, 256), jnp.float32)
    return call(final_kernel, (f32(4, 8, 8, 128), f32(3, 8, 8, 128)), (grid,), 11)(
        forces, cell, dest, elem, weight, state, ylo, yhi, ghosts, first, second
    )


def solution(mesh):
    return jax.shard_map(
        body,
        mesh=mesh,
        in_specs=(
            P(None, "gx", "gy", "gz"),
            P(("gx", "gy", "gz")),
            P(("gx", "gy", "gz"), None),
            P(("gx", "gy", "gz")),
            P(("gx", "gy", "gz")),
            P(None, ("gx", "gz")),
            P(("gx", "gz")),
        ),
        out_specs=(P(None, "gx", "gy", "gz"), P(None, "gx", "gy", "gz")),
        check_vma=False,
    )
```

```python
import jax
import jax.numpy as jnp
from jax import lax
from jax.experimental import pallas as pl
from jax.experimental.pallas import tpu as pltpu
from jax.sharding import PartitionSpec as P

DT_STEP = 0.4
BASE_COEF = 0.02
PRANDTL = 0.7
SMAG_COEF = 0.04

ROWS = 1024
PLANE = ("gy", "gz")


def call(kernel, outs, scratch=(), count=1, space=pltpu.VMEM, limit=24 * 1024 * 1024):
    return pl.pallas_call(
        kernel,
        out_shape=outs,
        in_specs=[pl.BlockSpec(memory_space=space)] * count,
        out_specs=jax.tree.map(lambda _: pl.BlockSpec(memory_space=pltpu.VMEM), outs),
        scratch_shapes=scratch,
        compiler_params=pltpu.CompilerParams(vmem_limit_bytes=limit),
        cost_estimate=pl.CostEstimate(
            flops=2_000_000, bytes_accessed=1_000_000, transcendentals=0
        ),
    )


def f32(*shape):
    return jax.ShapeDtypeStruct(shape, jnp.float32)


def halves(values):
    high = values.astype(jnp.bfloat16)
    return high, (values - high.astype(jnp.float32)).astype(jnp.bfloat16)


def onehot(index, size):
    wanted = lax.broadcasted_iota(jnp.int32, (size, ROWS), 0)
    return jnp.where(wanted == index, 1.0, 0.0).astype(jnp.bfloat16)


def pick(table, hot):
    both = jnp.concatenate(halves(table), axis=1)
    return jnp.dot(both, jnp.concatenate([hot, hot], axis=0), preferred_element_type=jnp.float32)


def put(values, hot):
    high, low = halves(values)
    dims = (((1,), (1,)), ((), ()))
    total = lax.dot_general(high, hot, dims, preferred_element_type=jnp.float32)
    return total + lax.dot_general(low, hot, dims, preferred_element_type=jnp.float32)


def cell_keys(cell):
    column = lax.broadcasted_iota(jnp.int32, (64, ROWS), 0) == (cell >> 7)
    return column, onehot(cell & 127, 128)


def element_keys(dest, elem):
    tile = (elem >> 4) * 4 + (dest & 3)
    along = dest >> 2
    number = tile * 2 + (along >> 3)
    shape = (32, 8, ROWS)
    row = lax.broadcasted_iota(jnp.int32, shape, 0) * 2 + (
        lax.broadcasted_iota(jnp.int32, shape, 1) & 1
    )
    return row == number[None], onehot((along & 7) * 16 + (elem & 15), 128)


def own_part(motion, coef):
    gx, gy = lax.axis_index("gx"), lax.axis_index("gy")
    row = lax.broadcasted_iota(jnp.int32, (8, 128), 0)
    lane = lax.broadcasted_iota(jnp.int32, (8, 128), 1)
    level = row >> 1
    held = jnp.where(
        level == 0,
        motion[0:1, :],
        jnp.where(level == 1, motion[1:2, :], jnp.where(level == 2, motion[2:3, :], coef[...])),
    )
    moved = pltpu.roll(held, ((gx & 7) * 16 - gy * 16 + 128) & 127, 1)
    mine = ((lane >> 4) == (gx & 7)) & ((row & 1) == (gx >> 3))
    return jnp.where(mine, moved, 0.0)


def lanes(count, places):
    row = lax.broadcasted_iota(jnp.int32, (count, 128), 0)
    lane = lax.broadcasted_iota(jnp.int32, (count, 128), 1)
    hot = (row == 0) & (lane == places[0])
    for i, place in enumerate(places[1:]):
        hot = hot | ((row == i + 1) & (lane == place))
    return jnp.where(hot, 1.0, 0.0)


def thirds(values):
    high, rest = halves(values)
    low = values - high.astype(jnp.float32) - rest.astype(jnp.float32)
    return high, rest, low.astype(jnp.bfloat16)


def take_lanes(places, rows):
    hot = lanes(8, places).astype(jnp.bfloat16)
    dims = (((1,), (1,)), ((), ()))
    parts = [
        lax.dot_general(hot, part, dims, preferred_element_type=jnp.float32)
        for part in thirds(rows)
    ]
    return parts[0] + parts[1] + parts[2]


def give_lanes(rows, places):
    hot = lanes(len(places), places)
    return lax.dot_general(
        jnp.concatenate(thirds(rows), axis=0),
        jnp.concatenate([hot, hot, hot], axis=0).astype(jnp.bfloat16),
        (((0,), (0,)), ((), ())),
        preferred_element_type=jnp.float32,
    )


def sample_kernel(
    state_in,
    cell_in,
    dest_in,
    elem_in,
    weight_in,
    motion_in,
    coef_in,
    out,
    own,
    yup,
    ydown,
    far,
    *scratch,
):
    held, sems = scratch[:7], scratch[7]
    sources = (state_in, cell_in, dest_in, elem_in, weight_in, motion_in, coef_in)
    copies = [
        pltpu.make_async_copy(source, target, sems.at[i])
        for i, (source, target) in enumerate(zip(sources, held))
    ]
    for copy in copies:
        copy.start()
    for copy in copies:
        copy.wait()
    state, cell, dest, elem, weight, motion, coef = held
    own[...] = own_part(motion, coef)
    yup[...] = state[:, :, 6:8]
    ydown[...] = state[:, :, 0:2]
    ends = take_lanes((0, 127, 1, 126), state[...].reshape(256, 128))
    blank = jnp.zeros((6, 128), jnp.float32)
    low, high, far_low, far_high = [
        jnp.concatenate([blank, ends[i : i + 1, 0:128], ends[i : i + 1, 128:256]], axis=0)
        for i in range(4)
    ]
    far[0], far[1] = far_low, far_high
    column, hot_z = cell_keys(cell[...])
    found = pick(state[0:3].reshape(192, 128), hot_z).reshape(3, 64, ROWS)
    sampled = [
        jnp.sum(jnp.where(column, found[c], 0.0), axis=0, keepdims=True) * weight[...]
        for c in range(3)
    ]
    row = lax.broadcasted_iota(jnp.int32, (8, ROWS), 0) >> 1
    pattern = jnp.where(
        row == 0, sampled[0], jnp.where(row == 1, sampled[1], jnp.where(row == 2, sampled[2], 0.0))
    )
    match, hot_lane = element_keys(dest[...], elem[...])
    spread = jnp.where(match, pattern[None], 0.0).reshape(256, ROWS)
    sums = put(spread, hot_lane).reshape(32, 8, 128)
    above = (lax.axis_index("gz") + 1) & 3
    for level in range(4):
        near = jnp.where(above == level, high, low)
        for across in range(level, 32, 4):
            out[across] = sums[across] + near


def total_kernel(parts, own, out):
    row = lax.broadcasted_iota(jnp.int32, (8, 128), 0)
    total = jnp.where(row < 6, jnp.sum(parts[...], axis=0), 0.0) + own[...]
    out[...] = jnp.broadcast_to(total[None], (16, 8, 128))


def force_kernel(parts, far, out):
    total = jnp.sum(parts[...], axis=0)
    row = lax.broadcasted_iota(jnp.int32, (8, 128), 0)

    def by_parity(values):
        values = values + pltpu.roll(values, 4, 0)
        return values + pltpu.roll(values, 2, 0)

    speed = jnp.sqrt(by_parity(jnp.where(row < 6, total * total, 0.0)))
    coef = by_parity(jnp.where(row < 6, 0.0, total))
    force = jnp.where(row < 6, -coef * speed * total, 0.0)
    above = (lax.axis_index("gz") + 1) & 3
    for level in range(4):
        block = force + jnp.where(above == level, far[1], far[0])
        for across in range(level, 32, 4):
            out[across] = block


def fill(grid, parts, state, ylo, yhi, ghosts, first, second):
    grid[:, 2:10, 0:8, 0:128] = state[...]
    grid[:, 2:10, 8:10, 0:128] = yhi[...]
    grid[:, 2:10, 14:16, 0:128] = ylo[...]
    far = jnp.concatenate([level_of(parts, 0, True), level_of(parts, 0, False)], axis=0)
    far = give_lanes(far, (1, 126)).reshape(4, 8, 8, 128)
    grid[:, 2:10, 0:8, 128:256] = ghosts[:, :, 0:8] + far
    grid[:, 2:10, 8:16, 128:256] = ghosts[:, :, 8:16]
    row = lax.broadcasted_iota(jnp.int32, (8, 128), 0)
    column = lax.broadcasted_iota(jnp.int32, (8, 128), 1)
    outer = (column == 0) | (column == 127)
    for plane, near, slab in (
        (0, 1, first[...]),
        (10, 10, second[...]),
    ):
        for c in range(4):
            grid[c, plane, 0:8, 0:128] = slab[2 * c]
            grid[c, plane + 1, 0:8, 0:128] = slab[2 * c + 1]
            over, under = slab[8, 2 * c : 2 * c + 1], slab[8, 2 * c + 1 : 2 * c + 2]
            grid[c, near, 8:16, 0:128] = jnp.where(row == 0, over, jnp.where(row == 7, under, 0.0))
            ends = slab[9] if c == 0 else pltpu.roll(slab[9], 128 - 2 * c, 1)
            grid[c, near, 0:8, 128:256] = jnp.where(outer, ends, 0.0)


def level_of(parts, across, up):
    gy, gz = lax.axis_index("gy"), lax.axis_index("gz")
    block = parts[((gy + across) & 7) * 4 + ((gz + (1 if up else 3)) & 3)]
    found = jnp.concatenate([block[6:7], block[7:8]], axis=1)
    return jnp.where(gz == (3 if up else 0), 0.0, found)


def faces_kernel(parts, state, ylo, yhi, first, second, ghosts):
    lane = lax.broadcasted_iota(jnp.int32, (1, 256), 1)

    def edge(up):
        y = lane & 7
        beside = jnp.where(y == 0, level_of(parts, 1, up), 0.0)
        return jnp.where(y == 7, level_of(parts, 7, up), beside)

    inner = jnp.concatenate([level_of(parts, 0, True), level_of(parts, 0, False)], axis=0)
    inner = give_lanes(inner, (0, 127)).reshape(4, 8, 8, 128)
    edges = jnp.concatenate([edge(True), edge(False)], axis=0)
    ghosts[:, :, 0:8] = inner
    ghosts[:, :, 8:16] = give_lanes(edges, (0, 127)).reshape(4, 8, 8, 128)

    column = lax.broadcasted_iota(jnp.int32, (8, 128), 1)
    outer = (column == 0) | (column == 127)

    def slab(x, near):
        tiles = [state[c, x + i] for c in range(4) for i in range(2)]
        across = [part[c, near, i : i + 1] for c in range(4) for part, i in ((yhi, 0), (ylo, 1))]
        ends = [jnp.where(outer, inner[c, near], 0.0) for c in range(4)]
        ends = [ends[0]] + [pltpu.roll(ends[c], 2 * c, 1) for c in range(1, 4)]
        return tiles + [jnp.concatenate(across, axis=0), ends[0] + ends[1] + ends[2] + ends[3]]

    for i, (high, low) in enumerate(zip(slab(6, 7), slab(0, 0))):
        first[i] = high
        second[i] = low


def final_kernel(
    parts, cell, dest, elem, weight, state, ylo, yhi, ghosts, first, second, *results
):
    new_state, body_force, grid = results
    match, hot_lane = element_keys(dest[...], elem[...])
    found = pick(parts[...].reshape(256, 128), hot_lane).reshape(32, 8, ROWS)
    pairs = jnp.sum(jnp.where(match, found, 0.0), axis=0)
    column, hot_z = cell_keys(cell[...])
    each = [(pairs[2 * c : 2 * c + 1] + pairs[2 * c + 1 : 2 * c + 2]) * weight[...] for c in range(3)]
    spread = jnp.concatenate([jnp.where(column, each[c], 0.0) for c in range(3)], axis=0)
    body = put(spread, hot_z).reshape(3, 8, 8, 128)
    body_force[...] = body

    gz = lax.axis_index("gz")
    fill(grid, parts, state, ylo, yhi, ghosts, first, second)
    level = lax.broadcasted_iota(jnp.int32, (1, 1, 256), 2)
    outside = ((level >= 128) & (level < 192) & (gz == 3)) | ((level >= 192) & (gz == 0))

    def around(values):
        return (
            (pltpu.roll(values, 15, 1), pltpu.roll(values, 1, 1)),
            (pltpu.roll(values, 255, 2), pltpu.roll(values, 1, 2)),
        )

    fields = [grid[c] for c in range(4)]
    sides = []
    diffs = []
    for c in range(4):
        middle = fields[c][1:11]
        near = ((fields[c][2:12], fields[c][0:10]),) + around(middle)
        sides.append(near)
        diffs.append([upper - lower for upper, lower in near])
    strain = 0.5 * (
        diffs[0][0] * diffs[0][0] + diffs[1][1] * diffs[1][1] + diffs[2][2] * diffs[2][2]
    )
    for i, j in ((0, 1), (0, 2), (1, 2)):
        paired = diffs[i][j] + diffs[j][i]
        strain = strain + 0.25 * paired * paired
    eddy = jnp.where(outside, 0.0, SMAG_COEF * jnp.sqrt(strain))

    def inner(values):
        return values[:, 0:8, 0:128]

    centre = inner(eddy[1:9])
    near = ((eddy[2:10], eddy[0:8]),) + around(eddy[1:9])
    faces = [[0.5 * (centre + inner(side)) for side in pair] for pair in near]
    wind = [0.5 * inner(fields[c][2:10]) for c in range(3)]
    for c in range(4):
        middle = inner(fields[c][2:10])
        ratio = 1.0 if c < 3 else 1.0 / PRANDTL
        change = 0.0
        for j in range(3):
            upper, lower = [inner(side[1:9]) for side in sides[c][j]]
            change = change + (BASE_COEF + ratio * faces[j][0]) * (upper - middle)
            change = change - (BASE_COEF + ratio * faces[j][1]) * (middle - lower)
            change = change - wind[j] * (upper - lower)
        if c < 3:
            change = change + body[c]
        new_state[c] = middle + DT_STEP * change


def shift(up, down, axis):
    count = lax.axis_size(axis)
    forward = [(i, (i + 1) % count) for i in range(count)]
    backward = [(target, source) for source, target in forward]
    return lax.ppermute(up, axis, forward), lax.ppermute(down, axis, backward)


def exchange(blocks, axes):
    return lax.all_to_all(blocks, axes, split_axis=0, concat_axis=0, tiled=True)


def body(state, sample_cell, sample_dest, sample_weight, sample_elem, element_motion, element_coef):
    cell = sample_cell.reshape(1, ROWS)
    dest = sample_dest.reshape(1, ROWS)
    elem = sample_elem.reshape(1, ROWS)
    weight = sample_weight.reshape(1, ROWS)

    coef = element_coef.reshape(1, 128)
    rows = pltpu.VMEM((1, ROWS), jnp.int32)
    held = (
        pltpu.VMEM((4, 8, 8, 128), jnp.float32),
        rows,
        rows,
        rows,
        pltpu.VMEM((1, ROWS), jnp.float32),
        pltpu.VMEM((3, 128), jnp.float32),
        pltpu.VMEM((1, 128), jnp.float32),
        pltpu.SemaphoreType.DMA((7,)),
    )
    side = f32(4, 8, 2, 128)
    partial, own, yup, ydown, far = call(
        sample_kernel,
        (f32(32, 8, 128), f32(8, 128), side, side, f32(2, 8, 128)),
        held,
        7,
        pltpu.HBM,
        60 * 1024 * 1024,
    )(state, cell, dest, elem, weight, element_motion, coef)
    parts = exchange(partial, PLANE)
    ylo, yhi = shift(yup, ydown, "gy")
    parts, ylo, yhi = lax.optimization_barrier((parts, ylo, yhi))

    totals = call(total_kernel, f32(16, 8, 128), count=2)(parts, own)
    totals = exchange(totals, "gx")
    slab = f32(10, 8, 128)
    first, second, ghosts = call(faces_kernel, (slab, slab, f32(4, 8, 16, 128)), count=4)(
        parts, state, ylo, yhi
    )
    first, second = shift(first, second, "gx")
    totals, first, second = lax.optimization_barrier((totals, first, second))

    forces = call(force_kernel, f32(32, 8, 128), count=2)(totals, far)
    forces = exchange(forces, PLANE)
    grid = pltpu.VMEM((4, 12, 16, 256), jnp.float32)
    return call(final_kernel, (f32(4, 8, 8, 128), f32(3, 8, 8, 128)), (grid,), 11)(
        forces, cell, dest, elem, weight, state, ylo, yhi, ghosts, first, second
    )


def solution(mesh):
    return jax.shard_map(
        body,
        mesh=mesh,
        in_specs=(
            P(None, "gx", "gy", "gz"),
            P(("gx", "gy", "gz")),
            P(("gx", "gy", "gz"), None),
            P(("gx", "gy", "gz")),
            P(("gx", "gy", "gz")),
            P(None, ("gx", "gz")),
            P(("gx", "gz")),
        ),
        out_specs=(P(None, "gx", "gy", "gz"), P(None, "gx", "gy", "gz")),
        check_vma=False,
    )
```

```python
import jax
import jax.numpy as jnp
from jax import lax
from jax.experimental import pallas as pl
from jax.experimental.pallas import tpu as pltpu
from jax.sharding import PartitionSpec as P

DT_STEP = 0.4
BASE_COEF = 0.02
PRANDTL = 0.7
SMAG_COEF = 0.04

ROWS = 1024
PLANE = ("gy", "gz")


def call(kernel, outs, scratch=(), count=1, space=pltpu.VMEM, limit=24 * 1024 * 1024):
    return pl.pallas_call(
        kernel,
        out_shape=outs,
        in_specs=[pl.BlockSpec(memory_space=space)] * count,
        out_specs=jax.tree.map(lambda _: pl.BlockSpec(memory_space=pltpu.VMEM), outs),
        scratch_shapes=scratch,
        compiler_params=pltpu.CompilerParams(vmem_limit_bytes=limit),
        cost_estimate=pl.CostEstimate(
            flops=2_000_000, bytes_accessed=1_000_000, transcendentals=0
        ),
    )


def f32(*shape):
    return jax.ShapeDtypeStruct(shape, jnp.float32)


def halves(values):
    high = values.astype(jnp.bfloat16)
    return high, (values - high.astype(jnp.float32)).astype(jnp.bfloat16)


def onehot(index, size):
    wanted = lax.broadcasted_iota(jnp.int32, (size, ROWS), 0)
    return jnp.where(wanted == index, 1.0, 0.0).astype(jnp.bfloat16)


def pick(table, hot):
    both = jnp.concatenate(halves(table), axis=1)
    return jnp.dot(both, jnp.concatenate([hot, hot], axis=0), preferred_element_type=jnp.float32)


def put(values, hot):
    high, low = halves(values)
    dims = (((1,), (1,)), ((), ()))
    total = lax.dot_general(high, hot, dims, preferred_element_type=jnp.float32)
    return total + lax.dot_general(low, hot, dims, preferred_element_type=jnp.float32)


def cell_keys(cell):
    column = lax.broadcasted_iota(jnp.int32, (64, ROWS), 0) == (cell >> 7)
    return column, onehot(cell & 127, 128)


def element_keys(dest, elem):
    tile = (elem >> 4) * 4 + (dest & 3)
    along = dest >> 2
    number = tile * 2 + (along >> 3)
    shape = (32, 8, ROWS)
    row = lax.broadcasted_iota(jnp.int32, shape, 0) * 2 + (
        lax.broadcasted_iota(jnp.int32, shape, 1) & 1
    )
    return row == number[None], onehot((along & 7) * 16 + (elem & 15), 128)


def own_part(motion, coef):
    gx, gy = lax.axis_index("gx"), lax.axis_index("gy")
    row = lax.broadcasted_iota(jnp.int32, (8, 128), 0)
    lane = lax.broadcasted_iota(jnp.int32, (8, 128), 1)
    level = row >> 1
    held = jnp.where(
        level == 0,
        motion[0:1, :],
        jnp.where(level == 1, motion[1:2, :], jnp.where(level == 2, motion[2:3, :], coef[...])),
    )
    moved = pltpu.roll(held, ((gx & 7) * 16 - gy * 16 + 128) & 127, 1)
    mine = ((lane >> 4) == (gx & 7)) & ((row & 1) == (gx >> 3))
    return jnp.where(mine, moved, 0.0)


def lanes(count, places):
    row = lax.broadcasted_iota(jnp.int32, (count, 128), 0)
    lane = lax.broadcasted_iota(jnp.int32, (count, 128), 1)
    hot = (row == 0) & (lane == places[0])
    for i, place in enumerate(places[1:]):
        hot = hot | ((row == i + 1) & (lane == place))
    return jnp.where(hot, 1.0, 0.0)


def thirds(values):
    high, rest = halves(values)
    low = values - high.astype(jnp.float32) - rest.astype(jnp.float32)
    return high, rest, low.astype(jnp.bfloat16)


def take_lanes(places, rows):
    hot = lanes(8, places).astype(jnp.bfloat16)
    dims = (((1,), (1,)), ((), ()))
    parts = [
        lax.dot_general(hot, part, dims, preferred_element_type=jnp.float32)
        for part in thirds(rows)
    ]
    return parts[0] + parts[1] + parts[2]


def give_lanes(rows, places):
    hot = lanes(len(places), places)
    return lax.dot_general(
        jnp.concatenate(thirds(rows), axis=0),
        jnp.concatenate([hot, hot, hot], axis=0).astype(jnp.bfloat16),
        (((0,), (0,)), ((), ())),
        preferred_element_type=jnp.float32,
    )


def sample_kernel(
    state_in,
    cell_in,
    dest_in,
    elem_in,
    weight_in,
    motion_in,
    coef_in,
    out,
    own,
    yup,
    ydown,
    far,
    *scratch,
):
    held, sems = scratch[:7], scratch[7]
    sources = (state_in, cell_in, dest_in, elem_in, weight_in, motion_in, coef_in)
    copies = [
        pltpu.make_async_copy(source, target, sems.at[i])
        for i, (source, target) in enumerate(zip(sources, held))
    ]
    for copy in copies:
        copy.start()
    for copy in copies:
        copy.wait()
    state, cell, dest, elem, weight, motion, coef = held
    own[...] = own_part(motion, coef)
    yup[...] = state[:, :, 6:8]
    ydown[...] = state[:, :, 0:2]
    ends = take_lanes((0, 127, 1, 126), state[...].reshape(256, 128))
    blank = jnp.zeros((6, 128), jnp.float32)
    low, high, far_low, far_high = [
        jnp.concatenate([blank, ends[i : i + 1, 0:128], ends[i : i + 1, 128:256]], axis=0)
        for i in range(4)
    ]
    far[0], far[1] = far_low, far_high
    column, hot_z = cell_keys(cell[...])
    found = pick(state[0:3].reshape(192, 128), hot_z).reshape(3, 64, ROWS)
    sampled = [
        jnp.sum(jnp.where(column, found[c], 0.0), axis=0, keepdims=True) * weight[...]
        for c in range(3)
    ]
    row = lax.broadcasted_iota(jnp.int32, (8, ROWS), 0) >> 1
    pattern = jnp.where(
        row == 0, sampled[0], jnp.where(row == 1, sampled[1], jnp.where(row == 2, sampled[2], 0.0))
    )
    match, hot_lane = element_keys(dest[...], elem[...])
    spread = jnp.where(match, pattern[None], 0.0).reshape(256, ROWS)
    sums = put(spread, hot_lane).reshape(32, 8, 128)
    above = (lax.axis_index("gz") + 1) & 3
    for level in range(4):
        near = jnp.where(above == level, high, low)
        for across in range(level, 32, 4):
            out[across] = sums[across] + near


def total_kernel(parts, own, out):
    row = lax.broadcasted_iota(jnp.int32, (8, 128), 0)
    total = jnp.where(row < 6, jnp.sum(parts[...], axis=0), 0.0) + own[...]
    out[...] = jnp.broadcast_to(total[None], (16, 8, 128))


def force_kernel(parts, far, out):
    total = jnp.sum(parts[...], axis=0)
    row = lax.broadcasted_iota(jnp.int32, (8, 128), 0)

    def by_parity(values):
        values = values + pltpu.roll(values, 4, 0)
        return values + pltpu.roll(values, 2, 0)

    speed = jnp.sqrt(by_parity(jnp.where(row < 6, total * total, 0.0)))
    coef = by_parity(jnp.where(row < 6, 0.0, total))
    force = jnp.where(row < 6, -coef * speed * total, 0.0)
    above = (lax.axis_index("gz") + 1) & 3
    for level in range(4):
        block = force + jnp.where(above == level, far[1], far[0])
        for across in range(level, 32, 4):
            out[across] = block


def fill(grid, parts, state, ylo, yhi, ghosts, first, second):
    grid[:, 2:10, 0:8, 0:128] = state[...]
    grid[:, 2:10, 8:10, 0:128] = yhi[...]
    grid[:, 2:10, 14:16, 0:128] = ylo[...]
    far = jnp.concatenate([level_of(parts, 0, True), level_of(parts, 0, False)], axis=0)
    far = give_lanes(far, (1, 126)).reshape(4, 8, 8, 128)
    grid[:, 2:10, 0:8, 128:256] = ghosts[:, :, 0:8] + far
    grid[:, 2:10, 8:16, 128:256] = ghosts[:, :, 8:16]
    row = lax.broadcasted_iota(jnp.int32, (8, 128), 0)
    column = lax.broadcasted_iota(jnp.int32, (8, 128), 1)
    outer = (column == 0) | (column == 127)
    for plane, near, slab in (
        (0, 1, first[...]),
        (10, 10, second[...]),
    ):
        for c in range(4):
            grid[c, plane, 0:8, 0:128] = slab[2 * c]
            grid[c, plane + 1, 0:8, 0:128] = slab[2 * c + 1]
            over, under = slab[8, 2 * c : 2 * c + 1], slab[8, 2 * c + 1 : 2 * c + 2]
            grid[c, near, 8:16, 0:128] = jnp.where(row == 0, over, jnp.where(row == 7, under, 0.0))
            ends = slab[9] if c == 0 else pltpu.roll(slab[9], 128 - 2 * c, 1)
            grid[c, near, 0:8, 128:256] = jnp.where(outer, ends, 0.0)


def level_of(parts, across, up):
    gy, gz = lax.axis_index("gy"), lax.axis_index("gz")
    block = parts[((gy + across) & 7) * 4 + ((gz + (1 if up else 3)) & 3)]
    found = jnp.concatenate([block[6:7], block[7:8]], axis=1)
    return jnp.where(gz == (3 if up else 0), 0.0, found)


def faces_kernel(parts, state, ylo, yhi, first, second, ghosts):
    lane = lax.broadcasted_iota(jnp.int32, (1, 256), 1)

    def edge(up):
        y = lane & 7
        beside = jnp.where(y == 0, level_of(parts, 1, up), 0.0)
        return jnp.where(y == 7, level_of(parts, 7, up), beside)

    inner = jnp.concatenate([level_of(parts, 0, True), level_of(parts, 0, False)], axis=0)
    inner = give_lanes(inner, (0, 127)).reshape(4, 8, 8, 128)
    edges = jnp.concatenate([edge(True), edge(False)], axis=0)
    ghosts[:, :, 0:8] = inner
    ghosts[:, :, 8:16] = give_lanes(edges, (0, 127)).reshape(4, 8, 8, 128)

    column = lax.broadcasted_iota(jnp.int32, (8, 128), 1)
    outer = (column == 0) | (column == 127)

    def slab(x, near):
        tiles = [state[c, x + i] for c in range(4) for i in range(2)]
        across = [part[c, near, i : i + 1] for c in range(4) for part, i in ((yhi, 0), (ylo, 1))]
        ends = [jnp.where(outer, inner[c, near], 0.0) for c in range(4)]
        ends = [ends[0]] + [pltpu.roll(ends[c], 2 * c, 1) for c in range(1, 4)]
        return tiles + [jnp.concatenate(across, axis=0), ends[0] + ends[1] + ends[2] + ends[3]]

    for i, (high, low) in enumerate(zip(slab(6, 7), slab(0, 0))):
        first[i] = high
        second[i] = low


def final_kernel(
    parts, cell, dest, elem, weight, state, ylo, yhi, ghosts, first, second, *results
):
    new_state, body_force, grid = results
    match, hot_lane = element_keys(dest[...], elem[...])
    found = pick(parts[...].reshape(256, 128), hot_lane).reshape(32, 8, ROWS)
    pairs = jnp.sum(jnp.where(match, found, 0.0), axis=0)
    column, hot_z = cell_keys(cell[...])
    each = [(pairs[2 * c : 2 * c + 1] + pairs[2 * c + 1 : 2 * c + 2]) * weight[...] for c in range(3)]
    spread = jnp.concatenate([jnp.where(column, each[c], 0.0) for c in range(3)], axis=0)
    body = put(spread, hot_z).reshape(3, 8, 8, 128)
    body_force[...] = body

    gz = lax.axis_index("gz")
    fill(grid, parts, state, ylo, yhi, ghosts, first, second)
    level = lax.broadcasted_iota(jnp.int32, (1, 1, 256), 2)
    outside = ((level >= 128) & (level < 192) & (gz == 3)) | ((level >= 192) & (gz == 0))

    def around(values):
        return (
            (pltpu.roll(values, 15, 1), pltpu.roll(values, 1, 1)),
            (pltpu.roll(values, 255, 2), pltpu.roll(values, 1, 2)),
        )

    fields = [grid[c] for c in range(4)]
    sides = []
    diffs = []
    for c in range(4):
        middle = fields[c][1:11]
        near = ((fields[c][2:12], fields[c][0:10]),) + around(middle)
        sides.append(near)
        diffs.append([upper - lower for upper, lower in near])
    strain = 0.5 * (
        diffs[0][0] * diffs[0][0] + diffs[1][1] * diffs[1][1] + diffs[2][2] * diffs[2][2]
    )
    for i, j in ((0, 1), (0, 2), (1, 2)):
        paired = diffs[i][j] + diffs[j][i]
        strain = strain + 0.25 * paired * paired
    eddy = jnp.where(outside, 0.0, SMAG_COEF * jnp.sqrt(strain))

    def inner(values):
        return values[:, 0:8, 0:128]

    centre = inner(eddy[1:9])
    near = ((eddy[2:10], eddy[0:8]),) + around(eddy[1:9])
    faces = [[0.5 * (centre + inner(side)) for side in pair] for pair in near]
    wind = [0.5 * inner(fields[c][2:10]) for c in range(3)]
    for c in range(4):
        middle = inner(fields[c][2:10])
        ratio = 1.0 if c < 3 else 1.0 / PRANDTL
        change = 0.0
        for j in range(3):
            upper, lower = [inner(side[1:9]) for side in sides[c][j]]
            change = change + (BASE_COEF + ratio * faces[j][0]) * (upper - middle)
            change = change - (BASE_COEF + ratio * faces[j][1]) * (middle - lower)
            change = change - wind[j] * (upper - lower)
        if c < 3:
            change = change + body[c]
        new_state[c] = middle + DT_STEP * change


def shift(up, down, axis):
    count = lax.axis_size(axis)
    forward = [(i, (i + 1) % count) for i in range(count)]
    backward = [(target, source) for source, target in forward]
    return lax.ppermute(up, axis, forward), lax.ppermute(down, axis, backward)


def exchange(blocks, axes, order=None):
    groups = None if order is None else [order]
    return lax.all_to_all(
        blocks, axes, split_axis=0, concat_axis=0, tiled=True, axis_index_groups=groups
    )


def body(state, sample_cell, sample_dest, sample_weight, sample_elem, element_motion, element_coef):
    cell = sample_cell.reshape(1, ROWS)
    dest = sample_dest.reshape(1, ROWS)
    elem = sample_elem.reshape(1, ROWS)
    weight = sample_weight.reshape(1, ROWS)

    coef = element_coef.reshape(1, 128)
    rows = pltpu.VMEM((1, ROWS), jnp.int32)
    held = (
        pltpu.VMEM((4, 8, 8, 128), jnp.float32),
        rows,
        rows,
        rows,
        pltpu.VMEM((1, ROWS), jnp.float32),
        pltpu.VMEM((3, 128), jnp.float32),
        pltpu.VMEM((1, 128), jnp.float32),
        pltpu.SemaphoreType.DMA((7,)),
    )
    side = f32(4, 8, 2, 128)
    partial, own, yup, ydown, far = call(
        sample_kernel,
        (f32(32, 8, 128), f32(8, 128), side, side, f32(2, 8, 128)),
        held,
        7,
        pltpu.HBM,
        60 * 1024 * 1024,
    )(state, cell, dest, elem, weight, element_motion, coef)
    parts = exchange(partial, PLANE)
    ylo, yhi = shift(yup, ydown, "gy")
    parts, ylo, yhi = lax.optimization_barrier((parts, ylo, yhi))

    totals = call(total_kernel, f32(16, 8, 128), count=2)(parts, own)
    totals = exchange(totals, "gx", [(i + 12) % 16 for i in range(16)])
    slab = f32(10, 8, 128)
    first, second, ghosts = call(faces_kernel, (slab, slab, f32(4, 8, 16, 128)), count=4)(
        parts, state, ylo, yhi
    )
    first, second = shift(first, second, "gx")
    totals, first, second = lax.optimization_barrier((totals, first, second))

    forces = call(force_kernel, f32(32, 8, 128), count=2)(totals, far)
    forces = exchange(forces, PLANE)
    grid = pltpu.VMEM((4, 12, 16, 256), jnp.float32)
    return call(final_kernel, (f32(4, 8, 8, 128), f32(3, 8, 8, 128)), (grid,), 11)(
        forces, cell, dest, elem, weight, state, ylo, yhi, ghosts, first, second
    )


def solution(mesh):
    return jax.shard_map(
        body,
        mesh=mesh,
        in_specs=(
            P(None, "gx", "gy", "gz"),
            P(("gx", "gy", "gz")),
            P(("gx", "gy", "gz"), None),
            P(("gx", "gy", "gz")),
            P(("gx", "gy", "gz")),
            P(None, ("gx", "gz")),
            P(("gx", "gz")),
        ),
        out_specs=(P(None, "gx", "gy", "gz"), P(None, "gx", "gy", "gz")),
        check_vma=False,
    )
```

```python
import jax
import jax.numpy as jnp
from jax import lax
from jax.experimental import pallas as pl
from jax.experimental.pallas import tpu as pltpu
from jax.sharding import PartitionSpec as P

DT_STEP = 0.4
BASE_COEF = 0.02
PRANDTL = 0.7
SMAG_COEF = 0.04

ROWS = 1024
PLANE = ("gy", "gz")
FIRST_TURN, ALONG_TURN, LAST_TURN = 22, 12, 18


def call(kernel, outs, scratch=(), count=1, space=pltpu.VMEM, limit=24 * 1024 * 1024):
    return pl.pallas_call(
        kernel,
        out_shape=outs,
        in_specs=[pl.BlockSpec(memory_space=space)] * count,
        out_specs=jax.tree.map(lambda _: pl.BlockSpec(memory_space=pltpu.VMEM), outs),
        scratch_shapes=scratch,
        compiler_params=pltpu.CompilerParams(vmem_limit_bytes=limit),
        cost_estimate=pl.CostEstimate(
            flops=2_000_000, bytes_accessed=1_000_000, transcendentals=0
        ),
    )


def f32(*shape):
    return jax.ShapeDtypeStruct(shape, jnp.float32)


def halves(values):
    high = values.astype(jnp.bfloat16)
    return high, (values - high.astype(jnp.float32)).astype(jnp.bfloat16)


def onehot(index, size):
    wanted = lax.broadcasted_iota(jnp.int32, (size, ROWS), 0)
    return jnp.where(wanted == index, 1.0, 0.0).astype(jnp.bfloat16)


def pick(table, hot):
    both = jnp.concatenate(halves(table), axis=1)
    return jnp.dot(both, jnp.concatenate([hot, hot], axis=0), preferred_element_type=jnp.float32)


def put(values, hot):
    high, low = halves(values)
    dims = (((1,), (1,)), ((), ()))
    total = lax.dot_general(high, hot, dims, preferred_element_type=jnp.float32)
    return total + lax.dot_general(low, hot, dims, preferred_element_type=jnp.float32)


def cell_keys(cell):
    column = lax.broadcasted_iota(jnp.int32, (64, ROWS), 0) == (cell >> 7)
    return column, onehot(cell & 127, 128)


def element_keys(dest, elem, turn):
    tile = ((elem >> 4) * 4 + (dest & 3)) ^ turn
    along = dest >> 2
    number = tile * 2 + (along >> 3)
    shape = (32, 8, ROWS)
    row = lax.broadcasted_iota(jnp.int32, shape, 0) * 2 + (
        lax.broadcasted_iota(jnp.int32, shape, 1) & 1
    )
    return row == number[None], onehot((along & 7) * 16 + (elem & 15), 128)


def own_part(motion, coef):
    gx, gy = lax.axis_index("gx"), lax.axis_index("gy")
    row = lax.broadcasted_iota(jnp.int32, (8, 128), 0)
    lane = lax.broadcasted_iota(jnp.int32, (8, 128), 1)
    level = row >> 1
    held = jnp.where(
        level == 0,
        motion[0:1, :],
        jnp.where(level == 1, motion[1:2, :], jnp.where(level == 2, motion[2:3, :], coef[...])),
    )
    moved = pltpu.roll(held, ((gx & 7) * 16 - gy * 16 + 128) & 127, 1)
    mine = ((lane >> 4) == (gx & 7)) & ((row & 1) == (gx >> 3))
    return jnp.where(mine, moved, 0.0)


def lanes(count, places):
    row = lax.broadcasted_iota(jnp.int32, (count, 128), 0)
    lane = lax.broadcasted_iota(jnp.int32, (count, 128), 1)
    hot = (row == 0) & (lane == places[0])
    for i, place in enumerate(places[1:]):
        hot = hot | ((row == i + 1) & (lane == place))
    return jnp.where(hot, 1.0, 0.0)


def thirds(values):
    high, rest = halves(values)
    low = values - high.astype(jnp.float32) - rest.astype(jnp.float32)
    return high, rest, low.astype(jnp.bfloat16)


def take_lanes(places, rows):
    hot = lanes(8, places).astype(jnp.bfloat16)
    dims = (((1,), (1,)), ((), ()))
    parts = [
        lax.dot_general(hot, part, dims, preferred_element_type=jnp.float32)
        for part in thirds(rows)
    ]
    return parts[0] + parts[1] + parts[2]


def give_lanes(rows, places):
    hot = lanes(len(places), places)
    return lax.dot_general(
        jnp.concatenate(thirds(rows), axis=0),
        jnp.concatenate([hot, hot, hot], axis=0).astype(jnp.bfloat16),
        (((0,), (0,)), ((), ())),
        preferred_element_type=jnp.float32,
    )


def sample_kernel(
    state_in,
    cell_in,
    dest_in,
    elem_in,
    weight_in,
    motion_in,
    coef_in,
    out,
    own,
    yup,
    ydown,
    far,
    *scratch,
):
    held, sems = scratch[:7], scratch[7]
    sources = (state_in, cell_in, dest_in, elem_in, weight_in, motion_in, coef_in)
    copies = [
        pltpu.make_async_copy(source, target, sems.at[i])
        for i, (source, target) in enumerate(zip(sources, held))
    ]
    for copy in copies:
        copy.start()
    for copy in copies:
        copy.wait()
    state, cell, dest, elem, weight, motion, coef = held
    own[...] = own_part(motion, coef)
    yup[...] = state[:, :, 6:8]
    ydown[...] = state[:, :, 0:2]
    ends = take_lanes((0, 127, 1, 126), state[...].reshape(256, 128))
    blank = jnp.zeros((6, 128), jnp.float32)
    low, high, far_low, far_high = [
        jnp.concatenate([blank, ends[i : i + 1, 0:128], ends[i : i + 1, 128:256]], axis=0)
        for i in range(4)
    ]
    far[0], far[1] = far_low, far_high
    column, hot_z = cell_keys(cell[...])
    found = pick(state[0:3].reshape(192, 128), hot_z).reshape(3, 64, ROWS)
    sampled = [
        jnp.sum(jnp.where(column, found[c], 0.0), axis=0, keepdims=True) * weight[...]
        for c in range(3)
    ]
    row = lax.broadcasted_iota(jnp.int32, (8, ROWS), 0) >> 1
    pattern = jnp.where(
        row == 0, sampled[0], jnp.where(row == 1, sampled[1], jnp.where(row == 2, sampled[2], 0.0))
    )
    match, hot_lane = element_keys(dest[...], elem[...], FIRST_TURN)
    spread = jnp.where(match, pattern[None], 0.0).reshape(256, ROWS)
    sums = put(spread, hot_lane).reshape(32, 8, 128)
    above = (lax.axis_index("gz") + 1) & 3
    for level in range(4):
        near = jnp.where(above == level, high, low)
        for across in range(level, 32, 4):
            out[across ^ FIRST_TURN] = sums[across ^ FIRST_TURN] + near


def total_kernel(parts, own, out):
    row = lax.broadcasted_iota(jnp.int32, (8, 128), 0)
    total = jnp.where(row < 6, jnp.sum(parts[...], axis=0), 0.0) + own[...]
    out[...] = jnp.broadcast_to(total[None], (16, 8, 128))


def force_kernel(parts, far, out):
    total = jnp.sum(parts[...], axis=0)
    row = lax.broadcasted_iota(jnp.int32, (8, 128), 0)

    def by_parity(values):
        values = values + pltpu.roll(values, 4, 0)
        return values + pltpu.roll(values, 2, 0)

    speed = jnp.sqrt(by_parity(jnp.where(row < 6, total * total, 0.0)))
    coef = by_parity(jnp.where(row < 6, 0.0, total))
    force = jnp.where(row < 6, -coef * speed * total, 0.0)
    above = (lax.axis_index("gz") + 1) & 3
    for level in range(4):
        block = force + jnp.where(above == level, far[1], far[0])
        for across in range(level, 32, 4):
            out[across ^ LAST_TURN] = block


def fill(grid, parts, state, ylo, yhi, ghosts, first, second):
    grid[:, 2:10, 0:8, 0:128] = state[...]
    grid[:, 2:10, 8:10, 0:128] = yhi[...]
    grid[:, 2:10, 14:16, 0:128] = ylo[...]
    far = [level_of(parts, 0, up, LAST_TURN) for up in (True, False)]
    far = jnp.concatenate(far, axis=0)
    far = give_lanes(far, (1, 126)).reshape(4, 8, 8, 128)
    grid[:, 2:10, 0:8, 128:256] = ghosts[:, :, 0:8] + far
    grid[:, 2:10, 8:16, 128:256] = ghosts[:, :, 8:16]
    row = lax.broadcasted_iota(jnp.int32, (8, 128), 0)
    column = lax.broadcasted_iota(jnp.int32, (8, 128), 1)
    outer = (column == 0) | (column == 127)
    for plane, near, slab in (
        (0, 1, first[...]),
        (10, 10, second[...]),
    ):
        for c in range(4):
            grid[c, plane, 0:8, 0:128] = slab[2 * c]
            grid[c, plane + 1, 0:8, 0:128] = slab[2 * c + 1]
            over, under = slab[8, 2 * c : 2 * c + 1], slab[8, 2 * c + 1 : 2 * c + 2]
            grid[c, near, 8:16, 0:128] = jnp.where(row == 0, over, jnp.where(row == 7, under, 0.0))
            ends = slab[9] if c == 0 else pltpu.roll(slab[9], 128 - 2 * c, 1)
            grid[c, near, 0:8, 128:256] = jnp.where(outer, ends, 0.0)


def level_of(parts, across, up, turn):
    gy, gz = lax.axis_index("gy"), lax.axis_index("gz")
    block = parts[(((gy + across) & 7) * 4 + ((gz + (1 if up else 3)) & 3)) ^ turn]
    found = jnp.concatenate([block[6:7], block[7:8]], axis=1)
    return jnp.where(gz == (3 if up else 0), 0.0, found)


def faces_kernel(parts, state, ylo, yhi, first, second, ghosts):
    lane = lax.broadcasted_iota(jnp.int32, (1, 256), 1)

    def edge(up):
        y = lane & 7
        beside = jnp.where(y == 0, level_of(parts, 1, up, FIRST_TURN), 0.0)
        return jnp.where(y == 7, level_of(parts, 7, up, FIRST_TURN), beside)

    inner = [level_of(parts, 0, up, FIRST_TURN) for up in (True, False)]
    inner = jnp.concatenate(inner, axis=0)
    inner = give_lanes(inner, (0, 127)).reshape(4, 8, 8, 128)
    edges = jnp.concatenate([edge(True), edge(False)], axis=0)
    ghosts[:, :, 0:8] = inner
    ghosts[:, :, 8:16] = give_lanes(edges, (0, 127)).reshape(4, 8, 8, 128)

    column = lax.broadcasted_iota(jnp.int32, (8, 128), 1)
    outer = (column == 0) | (column == 127)

    def slab(x, near):
        tiles = [state[c, x + i] for c in range(4) for i in range(2)]
        across = [part[c, near, i : i + 1] for c in range(4) for part, i in ((yhi, 0), (ylo, 1))]
        ends = [jnp.where(outer, inner[c, near], 0.0) for c in range(4)]
        ends = [ends[0]] + [pltpu.roll(ends[c], 2 * c, 1) for c in range(1, 4)]
        return tiles + [jnp.concatenate(across, axis=0), ends[0] + ends[1] + ends[2] + ends[3]]

    for i, (high, low) in enumerate(zip(slab(6, 7), slab(0, 0))):
        first[i] = high
        second[i] = low


def final_kernel(
    parts, cell, dest, elem, weight, state, ylo, yhi, ghosts, first, second, *results
):
    new_state, body_force, grid = results
    match, hot_lane = element_keys(dest[...], elem[...], LAST_TURN)
    found = pick(parts[...].reshape(256, 128), hot_lane).reshape(32, 8, ROWS)
    pairs = jnp.sum(jnp.where(match, found, 0.0), axis=0)
    column, hot_z = cell_keys(cell[...])
    each = [(pairs[2 * c : 2 * c + 1] + pairs[2 * c + 1 : 2 * c + 2]) * weight[...] for c in range(3)]
    spread = jnp.concatenate([jnp.where(column, each[c], 0.0) for c in range(3)], axis=0)
    body = put(spread, hot_z).reshape(3, 8, 8, 128)
    body_force[...] = body

    gz = lax.axis_index("gz")
    fill(grid, parts, state, ylo, yhi, ghosts, first, second)
    level = lax.broadcasted_iota(jnp.int32, (1, 1, 256), 2)
    outside = ((level >= 128) & (level < 192) & (gz == 3)) | ((level >= 192) & (gz == 0))

    def around(values):
        return (
            (pltpu.roll(values, 15, 1), pltpu.roll(values, 1, 1)),
            (pltpu.roll(values, 255, 2), pltpu.roll(values, 1, 2)),
        )

    fields = [grid[c] for c in range(4)]
    sides = []
    diffs = []
    for c in range(4):
        middle = fields[c][1:11]
        near = ((fields[c][2:12], fields[c][0:10]),) + around(middle)
        sides.append(near)
        diffs.append([upper - lower for upper, lower in near])
    strain = 0.5 * (
        diffs[0][0] * diffs[0][0] + diffs[1][1] * diffs[1][1] + diffs[2][2] * diffs[2][2]
    )
    for i, j in ((0, 1), (0, 2), (1, 2)):
        paired = diffs[i][j] + diffs[j][i]
        strain = strain + 0.25 * paired * paired
    eddy = jnp.where(outside, 0.0, SMAG_COEF * jnp.sqrt(strain))

    def inner(values):
        return values[:, 0:8, 0:128]

    centre = inner(eddy[1:9])
    near = ((eddy[2:10], eddy[0:8]),) + around(eddy[1:9])
    faces = [[0.5 * (centre + inner(side)) for side in pair] for pair in near]
    wind = [0.5 * inner(fields[c][2:10]) for c in range(3)]
    for c in range(4):
        middle = inner(fields[c][2:10])
        ratio = 1.0 if c < 3 else 1.0 / PRANDTL
        change = 0.0
        for j in range(3):
            upper, lower = [inner(side[1:9]) for side in sides[c][j]]
            change = change + (BASE_COEF + ratio * faces[j][0]) * (upper - middle)
            change = change - (BASE_COEF + ratio * faces[j][1]) * (middle - lower)
            change = change - wind[j] * (upper - lower)
        if c < 3:
            change = change + body[c]
        new_state[c] = middle + DT_STEP * change


def shift(up, down, axis):
    count = lax.axis_size(axis)
    forward = [(i, (i + 1) % count) for i in range(count)]
    backward = [(target, source) for source, target in forward]
    return lax.ppermute(up, axis, forward), lax.ppermute(down, axis, backward)


def exchange(blocks, axes, order):
    return lax.all_to_all(
        blocks, axes, split_axis=0, concat_axis=0, tiled=True, axis_index_groups=[order]
    )


def body(state, sample_cell, sample_dest, sample_weight, sample_elem, element_motion, element_coef):
    cell = sample_cell.reshape(1, ROWS)
    dest = sample_dest.reshape(1, ROWS)
    elem = sample_elem.reshape(1, ROWS)
    weight = sample_weight.reshape(1, ROWS)

    coef = element_coef.reshape(1, 128)
    rows = pltpu.VMEM((1, ROWS), jnp.int32)
    held = (
        pltpu.VMEM((4, 8, 8, 128), jnp.float32),
        rows,
        rows,
        rows,
        pltpu.VMEM((1, ROWS), jnp.float32),
        pltpu.VMEM((3, 128), jnp.float32),
        pltpu.VMEM((1, 128), jnp.float32),
        pltpu.SemaphoreType.DMA((7,)),
    )
    side = f32(4, 8, 2, 128)
    partial, own, yup, ydown, far = call(
        sample_kernel,
        (f32(32, 8, 128), f32(8, 128), side, side, f32(2, 8, 128)),
        held,
        7,
        pltpu.HBM,
        60 * 1024 * 1024,
    )(state, cell, dest, elem, weight, element_motion, coef)
    parts = exchange(partial, PLANE, [i ^ FIRST_TURN for i in range(32)])
    ylo, yhi = shift(yup, ydown, "gy")
    parts, ylo, yhi = lax.optimization_barrier((parts, ylo, yhi))

    totals = call(total_kernel, f32(16, 8, 128), count=2)(parts, own)
    totals = exchange(totals, "gx", [(i + ALONG_TURN) % 16 for i in range(16)])
    slab = f32(10, 8, 128)
    first, second, ghosts = call(faces_kernel, (slab, slab, f32(4, 8, 16, 128)), count=4)(
        parts, state, ylo, yhi
    )
    first, second = shift(first, second, "gx")
    totals, first, second = lax.optimization_barrier((totals, first, second))

    forces = call(force_kernel, f32(32, 8, 128), count=2)(totals, far)
    forces = exchange(forces, PLANE, [i ^ LAST_TURN for i in range(32)])
    grid = pltpu.VMEM((4, 12, 16, 256), jnp.float32)
    return call(final_kernel, (f32(4, 8, 8, 128), f32(3, 8, 8, 128)), (grid,), 11)(
        forces, cell, dest, elem, weight, state, ylo, yhi, ghosts, first, second
    )


def solution(mesh):
    return jax.shard_map(
        body,
        mesh=mesh,
        in_specs=(
            P(None, "gx", "gy", "gz"),
            P(("gx", "gy", "gz")),
            P(("gx", "gy", "gz"), None),
            P(("gx", "gy", "gz")),
            P(("gx", "gy", "gz")),
            P(None, ("gx", "gz")),
            P(("gx", "gz")),
        ),
        out_specs=(P(None, "gx", "gy", "gz"), P(None, "gx", "gy", "gz")),
        check_vma=False,
    )
```

```python
import jax
import jax.numpy as jnp
from jax import lax
from jax.experimental import pallas as pl
from jax.experimental.pallas import tpu as pltpu
from jax.sharding import PartitionSpec as P

DT_STEP = 0.4
BASE_COEF = 0.02
PRANDTL = 0.7
SMAG_COEF = 0.04

ROWS = 1024
PLANE = ("gy", "gz")
FIRST_TURN, ALONG_TURN, LAST_TURN = 22, 14, 18


def call(kernel, outs, scratch=(), count=1, space=pltpu.VMEM, limit=24 * 1024 * 1024):
    return pl.pallas_call(
        kernel,
        out_shape=outs,
        in_specs=[pl.BlockSpec(memory_space=space)] * count,
        out_specs=jax.tree.map(lambda _: pl.BlockSpec(memory_space=pltpu.VMEM), outs),
        scratch_shapes=scratch,
        compiler_params=pltpu.CompilerParams(vmem_limit_bytes=limit),
        cost_estimate=pl.CostEstimate(
            flops=2_000_000, bytes_accessed=1_000_000, transcendentals=0
        ),
    )


def f32(*shape):
    return jax.ShapeDtypeStruct(shape, jnp.float32)


def halves(values):
    high = values.astype(jnp.bfloat16)
    return high, (values - high.astype(jnp.float32)).astype(jnp.bfloat16)


def onehot(index, size):
    wanted = lax.broadcasted_iota(jnp.int32, (size, ROWS), 0)
    return jnp.where(wanted == index, 1.0, 0.0).astype(jnp.bfloat16)


def pick(table, hot):
    both = jnp.concatenate(halves(table), axis=1)
    return jnp.dot(both, jnp.concatenate([hot, hot], axis=0), preferred_element_type=jnp.float32)


def put(values, hot):
    high, low = halves(values)
    dims = (((1,), (1,)), ((), ()))
    total = lax.dot_general(high, hot, dims, preferred_element_type=jnp.float32)
    return total + lax.dot_general(low, hot, dims, preferred_element_type=jnp.float32)


def cell_keys(cell):
    column = lax.broadcasted_iota(jnp.int32, (64, ROWS), 0) == (cell >> 7)
    return column, onehot(cell & 127, 128)


def element_keys(dest, elem, turn):
    tile = ((elem >> 4) * 4 + (dest & 3)) ^ turn
    along = dest >> 2
    number = tile * 2 + (along >> 3)
    shape = (32, 8, ROWS)
    row = lax.broadcasted_iota(jnp.int32, shape, 0) * 2 + (
        lax.broadcasted_iota(jnp.int32, shape, 1) & 1
    )
    return row == number[None], onehot((along & 7) * 16 + (elem & 15), 128)


def own_part(motion, coef):
    gx, gy = lax.axis_index("gx"), lax.axis_index("gy")
    row = lax.broadcasted_iota(jnp.int32, (8, 128), 0)
    lane = lax.broadcasted_iota(jnp.int32, (8, 128), 1)
    level = row >> 1
    held = jnp.where(
        level == 0,
        motion[0:1, :],
        jnp.where(level == 1, motion[1:2, :], jnp.where(level == 2, motion[2:3, :], coef[...])),
    )
    moved = pltpu.roll(held, ((gx & 7) * 16 - gy * 16 + 128) & 127, 1)
    mine = ((lane >> 4) == (gx & 7)) & ((row & 1) == (gx >> 3))
    return jnp.where(mine, moved, 0.0)


def lanes(count, places):
    row = lax.broadcasted_iota(jnp.int32, (count, 128), 0)
    lane = lax.broadcasted_iota(jnp.int32, (count, 128), 1)
    hot = (row == 0) & (lane == places[0])
    for i, place in enumerate(places[1:]):
        hot = hot | ((row == i + 1) & (lane == place))
    return jnp.where(hot, 1.0, 0.0)


def thirds(values):
    high, rest = halves(values)
    low = values - high.astype(jnp.float32) - rest.astype(jnp.float32)
    return high, rest, low.astype(jnp.bfloat16)


def take_lanes(places, rows):
    hot = lanes(8, places).astype(jnp.bfloat16)
    dims = (((1,), (1,)), ((), ()))
    parts = [
        lax.dot_general(hot, part, dims, preferred_element_type=jnp.float32)
        for part in thirds(rows)
    ]
    return parts[0] + parts[1] + parts[2]


def give_lanes(rows, places):
    hot = lanes(len(places), places)
    return lax.dot_general(
        jnp.concatenate(thirds(rows), axis=0),
        jnp.concatenate([hot, hot, hot], axis=0).astype(jnp.bfloat16),
        (((0,), (0,)), ((), ())),
        preferred_element_type=jnp.float32,
    )


def sample_kernel(
    state_in,
    cell_in,
    dest_in,
    elem_in,
    weight_in,
    motion_in,
    coef_in,
    out,
    own,
    yup,
    ydown,
    far,
    *scratch,
):
    held, sems = scratch[:7], scratch[7]
    sources = (state_in, cell_in, dest_in, elem_in, weight_in, motion_in, coef_in)
    copies = [
        pltpu.make_async_copy(source, target, sems.at[i])
        for i, (source, target) in enumerate(zip(sources, held))
    ]
    for copy in copies:
        copy.start()
    for copy in copies:
        copy.wait()
    state, cell, dest, elem, weight, motion, coef = held
    own[...] = own_part(motion, coef)
    yup[...] = state[:, :, 6:8]
    ydown[...] = state[:, :, 0:2]
    ends = take_lanes((0, 127, 1, 126), state[...].reshape(256, 128))
    blank = jnp.zeros((6, 128), jnp.float32)
    low, high, far_low, far_high = [
        jnp.concatenate([blank, ends[i : i + 1, 0:128], ends[i : i + 1, 128:256]], axis=0)
        for i in range(4)
    ]
    far[0], far[1] = far_low, far_high
    column, hot_z = cell_keys(cell[...])
    found = pick(state[0:3].reshape(192, 128), hot_z).reshape(3, 64, ROWS)
    sampled = [
        jnp.sum(jnp.where(column, found[c], 0.0), axis=0, keepdims=True) * weight[...]
        for c in range(3)
    ]
    row = lax.broadcasted_iota(jnp.int32, (8, ROWS), 0) >> 1
    pattern = jnp.where(
        row == 0, sampled[0], jnp.where(row == 1, sampled[1], jnp.where(row == 2, sampled[2], 0.0))
    )
    match, hot_lane = element_keys(dest[...], elem[...], FIRST_TURN)
    spread = jnp.where(match, pattern[None], 0.0).reshape(256, ROWS)
    sums = put(spread, hot_lane).reshape(32, 8, 128)
    above = (lax.axis_index("gz") + 1) & 3
    for level in range(4):
        near = jnp.where(above == level, high, low)
        for across in range(level, 32, 4):
            out[across ^ FIRST_TURN] = sums[across ^ FIRST_TURN] + near


def total_kernel(parts, own, out):
    row = lax.broadcasted_iota(jnp.int32, (8, 128), 0)
    total = jnp.where(row < 6, jnp.sum(parts[...], axis=0), 0.0) + own[...]
    out[...] = jnp.broadcast_to(total[None], (16, 8, 128))


def force_kernel(parts, far, out):
    total = jnp.sum(parts[...], axis=0)
    row = lax.broadcasted_iota(jnp.int32, (8, 128), 0)

    def by_parity(values):
        values = values + pltpu.roll(values, 4, 0)
        return values + pltpu.roll(values, 2, 0)

    speed = jnp.sqrt(by_parity(jnp.where(row < 6, total * total, 0.0)))
    coef = by_parity(jnp.where(row < 6, 0.0, total))
    force = jnp.where(row < 6, -coef * speed * total, 0.0)
    above = (lax.axis_index("gz") + 1) & 3
    for level in range(4):
        block = force + jnp.where(above == level, far[1], far[0])
        for across in range(level, 32, 4):
            out[across ^ LAST_TURN] = block


def fill(grid, parts, state, ylo, yhi, ghosts, first, second):
    grid[:, 2:10, 0:8, 0:128] = state[...]
    grid[:, 2:10, 8:10, 0:128] = yhi[...]
    grid[:, 2:10, 14:16, 0:128] = ylo[...]
    far = [level_of(parts, 0, up, LAST_TURN) for up in (True, False)]
    far = jnp.concatenate(far, axis=0)
    far = give_lanes(far, (1, 126)).reshape(4, 8, 8, 128)
    grid[:, 2:10, 0:8, 128:256] = ghosts[:, :, 0:8] + far
    grid[:, 2:10, 8:16, 128:256] = ghosts[:, :, 8:16]
    row = lax.broadcasted_iota(jnp.int32, (8, 128), 0)
    column = lax.broadcasted_iota(jnp.int32, (8, 128), 1)
    outer = (column == 0) | (column == 127)
    for plane, near, slab in (
        (0, 1, first[...]),
        (10, 10, second[...]),
    ):
        for c in range(4):
            grid[c, plane, 0:8, 0:128] = slab[2 * c]
            grid[c, plane + 1, 0:8, 0:128] = slab[2 * c + 1]
            over, under = slab[8, 2 * c : 2 * c + 1], slab[8, 2 * c + 1 : 2 * c + 2]
            grid[c, near, 8:16, 0:128] = jnp.where(row == 0, over, jnp.where(row == 7, under, 0.0))
            ends = slab[9] if c == 0 else pltpu.roll(slab[9], 128 - 2 * c, 1)
            grid[c, near, 0:8, 128:256] = jnp.where(outer, ends, 0.0)


def level_of(parts, across, up, turn):
    gy, gz = lax.axis_index("gy"), lax.axis_index("gz")
    block = parts[(((gy + across) & 7) * 4 + ((gz + (1 if up else 3)) & 3)) ^ turn]
    found = jnp.concatenate([block[6:7], block[7:8]], axis=1)
    return jnp.where(gz == (3 if up else 0), 0.0, found)


def faces_kernel(parts, state, ylo, yhi, first, second, ghosts):
    lane = lax.broadcasted_iota(jnp.int32, (1, 256), 1)

    def edge(up):
        y = lane & 7
        beside = jnp.where(y == 0, level_of(parts, 1, up, FIRST_TURN), 0.0)
        return jnp.where(y == 7, level_of(parts, 7, up, FIRST_TURN), beside)

    inner = [level_of(parts, 0, up, FIRST_TURN) for up in (True, False)]
    inner = jnp.concatenate(inner, axis=0)
    inner = give_lanes(inner, (0, 127)).reshape(4, 8, 8, 128)
    edges = jnp.concatenate([edge(True), edge(False)], axis=0)
    ghosts[:, :, 0:8] = inner
    ghosts[:, :, 8:16] = give_lanes(edges, (0, 127)).reshape(4, 8, 8, 128)

    column = lax.broadcasted_iota(jnp.int32, (8, 128), 1)
    outer = (column == 0) | (column == 127)

    def slab(x, near):
        tiles = [state[c, x + i] for c in range(4) for i in range(2)]
        across = [part[c, near, i : i + 1] for c in range(4) for part, i in ((yhi, 0), (ylo, 1))]
        ends = [jnp.where(outer, inner[c, near], 0.0) for c in range(4)]
        ends = [ends[0]] + [pltpu.roll(ends[c], 2 * c, 1) for c in range(1, 4)]
        return tiles + [jnp.concatenate(across, axis=0), ends[0] + ends[1] + ends[2] + ends[3]]

    for i, (high, low) in enumerate(zip(slab(6, 7), slab(0, 0))):
        first[i] = high
        second[i] = low


def final_kernel(
    parts, cell, dest, elem, weight, state, ylo, yhi, ghosts, first, second, *results
):
    new_state, body_force, grid = results
    match, hot_lane = element_keys(dest[...], elem[...], LAST_TURN)
    found = pick(parts[...].reshape(256, 128), hot_lane).reshape(32, 8, ROWS)
    pairs = jnp.sum(jnp.where(match, found, 0.0), axis=0)
    column, hot_z = cell_keys(cell[...])
    each = [(pairs[2 * c : 2 * c + 1] + pairs[2 * c + 1 : 2 * c + 2]) * weight[...] for c in range(3)]
    spread = jnp.concatenate([jnp.where(column, each[c], 0.0) for c in range(3)], axis=0)
    body = put(spread, hot_z).reshape(3, 8, 8, 128)
    body_force[...] = body

    gz = lax.axis_index("gz")
    fill(grid, parts, state, ylo, yhi, ghosts, first, second)
    level = lax.broadcasted_iota(jnp.int32, (1, 1, 256), 2)
    outside = ((level >= 128) & (level < 192) & (gz == 3)) | ((level >= 192) & (gz == 0))

    def around(values):
        return (
            (pltpu.roll(values, 15, 1), pltpu.roll(values, 1, 1)),
            (pltpu.roll(values, 255, 2), pltpu.roll(values, 1, 2)),
        )

    fields = [grid[c] for c in range(4)]
    sides = []
    diffs = []
    for c in range(4):
        middle = fields[c][1:11]
        near = ((fields[c][2:12], fields[c][0:10]),) + around(middle)
        sides.append(near)
        diffs.append([upper - lower for upper, lower in near])
    strain = 0.5 * (
        diffs[0][0] * diffs[0][0] + diffs[1][1] * diffs[1][1] + diffs[2][2] * diffs[2][2]
    )
    for i, j in ((0, 1), (0, 2), (1, 2)):
        paired = diffs[i][j] + diffs[j][i]
        strain = strain + 0.25 * paired * paired
    eddy = jnp.where(outside, 0.0, SMAG_COEF * jnp.sqrt(strain))

    def inner(values):
        return values[:, 0:8, 0:128]

    centre = inner(eddy[1:9])
    near = ((eddy[2:10], eddy[0:8]),) + around(eddy[1:9])
    faces = [[0.5 * (centre + inner(side)) for side in pair] for pair in near]
    wind = [0.5 * inner(fields[c][2:10]) for c in range(3)]
    for c in range(4):
        middle = inner(fields[c][2:10])
        ratio = 1.0 if c < 3 else 1.0 / PRANDTL
        change = 0.0
        for j in range(3):
            upper, lower = [inner(side[1:9]) for side in sides[c][j]]
            change = change + (BASE_COEF + ratio * faces[j][0]) * (upper - middle)
            change = change - (BASE_COEF + ratio * faces[j][1]) * (middle - lower)
            change = change - wind[j] * (upper - lower)
        if c < 3:
            change = change + body[c]
        new_state[c] = middle + DT_STEP * change


def shift(up, down, axis):
    count = lax.axis_size(axis)
    forward = [(i, (i + 1) % count) for i in range(count)]
    backward = [(target, source) for source, target in forward]
    return lax.ppermute(up, axis, forward), lax.ppermute(down, axis, backward)


def exchange(blocks, axes, order):
    return lax.all_to_all(
        blocks, axes, split_axis=0, concat_axis=0, tiled=True, axis_index_groups=[order]
    )


def body(state, sample_cell, sample_dest, sample_weight, sample_elem, element_motion, element_coef):
    cell = sample_cell.reshape(1, ROWS)
    dest = sample_dest.reshape(1, ROWS)
    elem = sample_elem.reshape(1, ROWS)
    weight = sample_weight.reshape(1, ROWS)

    coef = element_coef.reshape(1, 128)
    rows = pltpu.VMEM((1, ROWS), jnp.int32)
    held = (
        pltpu.VMEM((4, 8, 8, 128), jnp.float32),
        rows,
        rows,
        rows,
        pltpu.VMEM((1, ROWS), jnp.float32),
        pltpu.VMEM((3, 128), jnp.float32),
        pltpu.VMEM((1, 128), jnp.float32),
        pltpu.SemaphoreType.DMA((7,)),
    )
    side = f32(4, 8, 2, 128)
    partial, own, yup, ydown, far = call(
        sample_kernel,
        (f32(32, 8, 128), f32(8, 128), side, side, f32(2, 8, 128)),
        held,
        7,
        pltpu.HBM,
        60 * 1024 * 1024,
    )(state, cell, dest, elem, weight, element_motion, coef)
    parts = exchange(partial, PLANE, [i ^ FIRST_TURN for i in range(32)])
    ylo, yhi = shift(yup, ydown, "gy")
    parts, ylo, yhi = lax.optimization_barrier((parts, ylo, yhi))

    totals = call(total_kernel, f32(16, 8, 128), count=2)(parts, own)
    totals = exchange(totals, "gx", [(i + ALONG_TURN) % 16 for i in range(16)])
    slab = f32(10, 8, 128)
    first, second, ghosts = call(faces_kernel, (slab, slab, f32(4, 8, 16, 128)), count=4)(
        parts, state, ylo, yhi
    )
    first, second = shift(first, second, "gx")
    totals, first, second = lax.optimization_barrier((totals, first, second))

    forces = call(force_kernel, f32(32, 8, 128), count=2)(totals, far)
    forces = exchange(forces, PLANE, [i ^ LAST_TURN for i in range(32)])
    grid = pltpu.VMEM((4, 12, 16, 256), jnp.float32)
    return call(final_kernel, (f32(4, 8, 8, 128), f32(3, 8, 8, 128)), (grid,), 11)(
        forces, cell, dest, elem, weight, state, ylo, yhi, ghosts, first, second
    )


def solution(mesh):
    return jax.shard_map(
        body,
        mesh=mesh,
        in_specs=(
            P(None, "gx", "gy", "gz"),
            P(("gx", "gy", "gz")),
            P(("gx", "gy", "gz"), None),
            P(("gx", "gy", "gz")),
            P(("gx", "gy", "gz")),
            P(None, ("gx", "gz")),
            P(("gx", "gz")),
        ),
        out_specs=(P(None, "gx", "gy", "gz"), P(None, "gx", "gy", "gz")),
        check_vma=False,
    )
```

```python
import jax
import jax.numpy as jnp
from jax import lax
from jax.experimental import pallas as pl
from jax.experimental.pallas import tpu as pltpu
from jax.sharding import PartitionSpec as P

DT_STEP = 0.4
BASE_COEF = 0.02
PRANDTL = 0.7
SMAG_COEF = 0.04

ROWS = 1024
PLANE = ("gy", "gz")
FIRST_TURN, ALONG_TURN, LAST_TURN = 22, 14, 18


def call(kernel, outs, scratch=(), count=1, space=pltpu.VMEM, limit=24 * 1024 * 1024):
    return pl.pallas_call(
        kernel,
        out_shape=outs,
        in_specs=[pl.BlockSpec(memory_space=space)] * count,
        out_specs=jax.tree.map(lambda _: pl.BlockSpec(memory_space=pltpu.VMEM), outs),
        scratch_shapes=scratch,
        compiler_params=pltpu.CompilerParams(vmem_limit_bytes=limit),
        cost_estimate=pl.CostEstimate(
            flops=2_000_000, bytes_accessed=1_000_000, transcendentals=0
        ),
    )


def f32(*shape):
    return jax.ShapeDtypeStruct(shape, jnp.float32)


def halves(values):
    high = values.astype(jnp.bfloat16)
    return high, (values - high.astype(jnp.float32)).astype(jnp.bfloat16)


def onehot(index, size):
    wanted = lax.broadcasted_iota(jnp.int32, (size, ROWS), 0)
    return jnp.where(wanted == index, 1.0, 0.0).astype(jnp.bfloat16)


def pick(table, hot):
    both = jnp.concatenate(halves(table), axis=1)
    return jnp.dot(both, jnp.concatenate([hot, hot], axis=0), preferred_element_type=jnp.float32)


def put(values, hot):
    high, low = halves(values)
    dims = (((1,), (1,)), ((), ()))
    total = lax.dot_general(high, hot, dims, preferred_element_type=jnp.float32)
    return total + lax.dot_general(low, hot, dims, preferred_element_type=jnp.float32)


def cell_keys(cell):
    column = lax.broadcasted_iota(jnp.int32, (64, ROWS), 0) == (cell >> 7)
    return column, onehot(cell & 127, 128)


def element_keys(dest, elem, turn):
    tile = ((elem >> 4) * 4 + (dest & 3)) ^ turn
    along = dest >> 2
    number = tile * 2 + (along >> 3)
    shape = (32, 8, ROWS)
    row = lax.broadcasted_iota(jnp.int32, shape, 0) * 2 + (
        lax.broadcasted_iota(jnp.int32, shape, 1) & 1
    )
    return row == number[None], onehot((along & 7) * 16 + (elem & 15), 128)


def own_part(motion, coef):
    gx, gy = lax.axis_index("gx"), lax.axis_index("gy")
    row = lax.broadcasted_iota(jnp.int32, (8, 128), 0)
    lane = lax.broadcasted_iota(jnp.int32, (8, 128), 1)
    level = row >> 1
    held = jnp.where(
        level == 0,
        motion[0:1, :],
        jnp.where(level == 1, motion[1:2, :], jnp.where(level == 2, motion[2:3, :], coef[...])),
    )
    moved = pltpu.roll(held, ((gx & 7) * 16 - gy * 16 + 128) & 127, 1)
    mine = ((lane >> 4) == (gx & 7)) & ((row & 1) == (gx >> 3))
    return jnp.where(mine, moved, 0.0)


def lanes(count, places):
    row = lax.broadcasted_iota(jnp.int32, (count, 128), 0)
    lane = lax.broadcasted_iota(jnp.int32, (count, 128), 1)
    hot = (row == 0) & (lane == places[0])
    for i, place in enumerate(places[1:]):
        hot = hot | ((row == i + 1) & (lane == place))
    return jnp.where(hot, 1.0, 0.0)


def thirds(values):
    high, rest = halves(values)
    low = values - high.astype(jnp.float32) - rest.astype(jnp.float32)
    return high, rest, low.astype(jnp.bfloat16)


def take_lanes(places, rows):
    hot = lanes(8, places).astype(jnp.bfloat16)
    dims = (((1,), (1,)), ((), ()))
    parts = [
        lax.dot_general(hot, part, dims, preferred_element_type=jnp.float32)
        for part in thirds(rows)
    ]
    return parts[0] + parts[1] + parts[2]


def give_lanes(rows, places):
    hot = lanes(len(places), places)
    return lax.dot_general(
        jnp.concatenate(thirds(rows), axis=0),
        jnp.concatenate([hot, hot, hot], axis=0).astype(jnp.bfloat16),
        (((0,), (0,)), ((), ())),
        preferred_element_type=jnp.float32,
    )


def sample_kernel(
    state_in,
    cell_in,
    dest_in,
    elem_in,
    weight_in,
    motion_in,
    coef_in,
    out,
    own,
    yup,
    ydown,
    far,
    *scratch,
):
    held, sems = scratch[:7], scratch[7]
    sources = (state_in, cell_in, dest_in, elem_in, weight_in, motion_in, coef_in)
    copies = [
        pltpu.make_async_copy(source, target, sems.at[i])
        for i, (source, target) in enumerate(zip(sources, held))
    ]
    for copy in copies:
        copy.start()
    for copy in copies:
        copy.wait()
    state, cell, dest, elem, weight, motion, coef = held
    own[...] = own_part(motion, coef)
    yup[...] = state[:, :, 6:8]
    ydown[...] = state[:, :, 0:2]
    ends = take_lanes((0, 127, 1, 126), state[...].reshape(256, 128))
    blank = jnp.zeros((6, 128), jnp.float32)
    low, high, far_low, far_high = [
        jnp.concatenate([blank, ends[i : i + 1, 0:128], ends[i : i + 1, 128:256]], axis=0)
        for i in range(4)
    ]
    far[0], far[1] = far_low, far_high
    column, hot_z = cell_keys(cell[...])
    found = pick(state[0:3].reshape(192, 128), hot_z).reshape(3, 64, ROWS)
    sampled = [
        jnp.sum(jnp.where(column, found[c], 0.0), axis=0, keepdims=True) * weight[...]
        for c in range(3)
    ]
    row = lax.broadcasted_iota(jnp.int32, (8, ROWS), 0) >> 1
    pattern = jnp.where(
        row == 0, sampled[0], jnp.where(row == 1, sampled[1], jnp.where(row == 2, sampled[2], 0.0))
    )
    match, hot_lane = element_keys(dest[...], elem[...], FIRST_TURN)
    spread = jnp.where(match, pattern[None], 0.0).reshape(256, ROWS)
    sums = put(spread, hot_lane).reshape(32, 8, 128)
    above = (lax.axis_index("gz") + 1) & 3
    for level in range(4):
        near = jnp.where(above == level, high, low)
        for across in range(level, 32, 4):
            out[across ^ FIRST_TURN] = sums[across ^ FIRST_TURN] + near


def total_kernel(parts, own, out):
    row = lax.broadcasted_iota(jnp.int32, (8, 128), 0)
    total = jnp.where(row < 6, jnp.sum(parts[...], axis=0), 0.0) + own[...]
    out[...] = jnp.broadcast_to(total[None], (16, 8, 128))


def force_kernel(parts, far, out):
    total = jnp.sum(parts[...], axis=0)
    row = lax.broadcasted_iota(jnp.int32, (8, 128), 0)

    def by_parity(values):
        values = values + pltpu.roll(values, 4, 0)
        return values + pltpu.roll(values, 2, 0)

    speed = jnp.sqrt(by_parity(jnp.where(row < 6, total * total, 0.0)))
    coef = by_parity(jnp.where(row < 6, 0.0, total))
    force = jnp.where(row < 6, -coef * speed * total, 0.0)
    above = (lax.axis_index("gz") + 1) & 3
    for level in range(4):
        block = force + jnp.where(above == level, far[1], far[0])
        for across in range(level, 32, 4):
            out[across ^ LAST_TURN] = block


def fill(grid, parts, state, ylo, yhi, ghosts, first, second):
    grid[:, 2:10, 0:8, 0:128] = state[...]
    grid[:, 2:10, 8:10, 0:128] = yhi[...]
    grid[:, 2:10, 14:16, 0:128] = ylo[...]
    far = [level_of(parts, 0, up, LAST_TURN) for up in (True, False)]
    far = jnp.concatenate(far, axis=0)
    far = give_lanes(far, (1, 126)).reshape(4, 8, 8, 128)
    grid[:, 2:10, 0:8, 128:256] = ghosts[:, :, 0:8] + far
    grid[:, 2:10, 8:16, 128:256] = ghosts[:, :, 8:16]
    row = lax.broadcasted_iota(jnp.int32, (8, 128), 0)
    column = lax.broadcasted_iota(jnp.int32, (8, 128), 1)
    outer = (column == 0) | (column == 127)
    for plane, near, slab in (
        (0, 1, first[...]),
        (10, 10, second[...]),
    ):
        for c in range(4):
            grid[c, plane, 0:8, 0:128] = slab[2 * c]
            grid[c, plane + 1, 0:8, 0:128] = slab[2 * c + 1]
            over, under = slab[8, 2 * c : 2 * c + 1], slab[8, 2 * c + 1 : 2 * c + 2]
            grid[c, near, 8:16, 0:128] = jnp.where(row == 0, over, jnp.where(row == 7, under, 0.0))
            ends = slab[9] if c == 0 else pltpu.roll(slab[9], 128 - 2 * c, 1)
            grid[c, near, 0:8, 128:256] = jnp.where(outer, ends, 0.0)


def level_of(parts, across, up, turn):
    gy, gz = lax.axis_index("gy"), lax.axis_index("gz")
    block = parts[(((gy + across) & 7) * 4 + ((gz + (1 if up else 3)) & 3)) ^ turn]
    found = jnp.concatenate([block[6:7], block[7:8]], axis=1)
    return jnp.where(gz == (3 if up else 0), 0.0, found)


def faces_kernel(parts, state, ylo, yhi, first, second, ghosts):
    lane = lax.broadcasted_iota(jnp.int32, (1, 256), 1)

    def edge(up):
        y = lane & 7
        beside = jnp.where(y == 0, level_of(parts, 1, up, FIRST_TURN), 0.0)
        return jnp.where(y == 7, level_of(parts, 7, up, FIRST_TURN), beside)

    inner = [level_of(parts, 0, up, FIRST_TURN) for up in (True, False)]
    inner = jnp.concatenate(inner, axis=0)
    inner = give_lanes(inner, (0, 127)).reshape(4, 8, 8, 128)
    edges = jnp.concatenate([edge(True), edge(False)], axis=0)
    ghosts[:, :, 0:8] = inner
    ghosts[:, :, 8:16] = give_lanes(edges, (0, 127)).reshape(4, 8, 8, 128)

    def slab(x, near):
        tiles = [state[c, x + i] for c in range(4) for i in range(2)]
        across = [part[c, near, i : i + 1] for c in range(4) for part, i in ((yhi, 0), (ylo, 1))]
        ends = [inner[c, near] for c in range(4)]
        ends = [ends[0]] + [pltpu.roll(ends[c], 2 * c, 1) for c in range(1, 4)]
        return tiles + [jnp.concatenate(across, axis=0), ends[0] + ends[1] + ends[2] + ends[3]]

    for i, (high, low) in enumerate(zip(slab(6, 7), slab(0, 0))):
        first[i] = high
        second[i] = low


def final_kernel(
    parts, cell, dest, elem, weight, state, ylo, yhi, ghosts, first, second, *results
):
    new_state, body_force, grid = results
    match, hot_lane = element_keys(dest[...], elem[...], LAST_TURN)
    found = pick(parts[...].reshape(256, 128), hot_lane).reshape(32, 8, ROWS)
    pairs = jnp.sum(jnp.where(match, found, 0.0), axis=0)
    column, hot_z = cell_keys(cell[...])
    each = [(pairs[2 * c : 2 * c + 1] + pairs[2 * c + 1 : 2 * c + 2]) * weight[...] for c in range(3)]
    spread = jnp.concatenate([jnp.where(column, each[c], 0.0) for c in range(3)], axis=0)
    body = put(spread, hot_z).reshape(3, 8, 8, 128)
    body_force[...] = body

    gz = lax.axis_index("gz")
    fill(grid, parts, state, ylo, yhi, ghosts, first, second)
    level = lax.broadcasted_iota(jnp.int32, (1, 1, 256), 2)
    outside = ((level >= 128) & (level < 192) & (gz == 3)) | ((level >= 192) & (gz == 0))

    def around(values):
        return (
            (pltpu.roll(values, 15, 1), pltpu.roll(values, 1, 1)),
            (pltpu.roll(values, 255, 2), pltpu.roll(values, 1, 2)),
        )

    fields = [grid[c] for c in range(4)]
    sides = []
    diffs = []
    for c in range(4):
        middle = fields[c][1:11]
        near = ((fields[c][2:12], fields[c][0:10]),) + around(middle)
        sides.append(near)
        diffs.append([upper - lower for upper, lower in near])
    strain = 0.5 * (
        diffs[0][0] * diffs[0][0] + diffs[1][1] * diffs[1][1] + diffs[2][2] * diffs[2][2]
    )
    for i, j in ((0, 1), (0, 2), (1, 2)):
        paired = diffs[i][j] + diffs[j][i]
        strain = strain + 0.25 * paired * paired
    eddy = jnp.where(outside, 0.0, SMAG_COEF * jnp.sqrt(strain))

    def inner(values):
        return values[:, 0:8, 0:128]

    centre = inner(eddy[1:9])
    near = ((eddy[2:10], eddy[0:8]),) + around(eddy[1:9])
    faces = [[0.5 * (centre + inner(side)) for side in pair] for pair in near]
    wind = [0.5 * inner(fields[c][2:10]) for c in range(3)]
    for c in range(4):
        middle = inner(fields[c][2:10])
        ratio = 1.0 if c < 3 else 1.0 / PRANDTL
        change = 0.0
        for j in range(3):
            upper, lower = [inner(side[1:9]) for side in sides[c][j]]
            change = change + (BASE_COEF + ratio * faces[j][0]) * (upper - middle)
            change = change - (BASE_COEF + ratio * faces[j][1]) * (middle - lower)
            change = change - wind[j] * (upper - lower)
        if c < 3:
            change = change + body[c]
        new_state[c] = middle + DT_STEP * change


def shift(up, down, axis):
    count = lax.axis_size(axis)
    forward = [(i, (i + 1) % count) for i in range(count)]
    backward = [(target, source) for source, target in forward]
    return lax.ppermute(up, axis, forward), lax.ppermute(down, axis, backward)


def exchange(blocks, axes, order):
    return lax.all_to_all(
        blocks, axes, split_axis=0, concat_axis=0, tiled=True, axis_index_groups=[order]
    )


def body(state, sample_cell, sample_dest, sample_weight, sample_elem, element_motion, element_coef):
    cell = sample_cell.reshape(1, ROWS)
    dest = sample_dest.reshape(1, ROWS)
    elem = sample_elem.reshape(1, ROWS)
    weight = sample_weight.reshape(1, ROWS)

    coef = element_coef.reshape(1, 128)
    rows = pltpu.VMEM((1, ROWS), jnp.int32)
    held = (
        pltpu.VMEM((4, 8, 8, 128), jnp.float32),
        rows,
        rows,
        rows,
        pltpu.VMEM((1, ROWS), jnp.float32),
        pltpu.VMEM((3, 128), jnp.float32),
        pltpu.VMEM((1, 128), jnp.float32),
        pltpu.SemaphoreType.DMA((7,)),
    )
    side = f32(4, 8, 2, 128)
    partial, own, yup, ydown, far = call(
        sample_kernel,
        (f32(32, 8, 128), f32(8, 128), side, side, f32(2, 8, 128)),
        held,
        7,
        pltpu.HBM,
        60 * 1024 * 1024,
    )(state, cell, dest, elem, weight, element_motion, coef)
    parts = exchange(partial, PLANE, [i ^ FIRST_TURN for i in range(32)])
    ylo, yhi = shift(yup, ydown, "gy")
    parts, ylo, yhi = lax.optimization_barrier((parts, ylo, yhi))

    totals = call(total_kernel, f32(16, 8, 128), count=2)(parts, own)
    totals = exchange(totals, "gx", [(i + ALONG_TURN) % 16 for i in range(16)])
    slab = f32(10, 8, 128)
    first, second, ghosts = call(faces_kernel, (slab, slab, f32(4, 8, 16, 128)), count=4)(
        parts, state, ylo, yhi
    )
    first, second = shift(first, second, "gx")
    totals, first, second = lax.optimization_barrier((totals, first, second))

    forces = call(force_kernel, f32(32, 8, 128), count=2)(totals, far)
    forces = exchange(forces, PLANE, [i ^ LAST_TURN for i in range(32)])
    grid = pltpu.VMEM((4, 12, 16, 256), jnp.float32)
    return call(final_kernel, (f32(4, 8, 8, 128), f32(3, 8, 8, 128)), (grid,), 11)(
        forces, cell, dest, elem, weight, state, ylo, yhi, ghosts, first, second
    )


def solution(mesh):
    return jax.shard_map(
        body,
        mesh=mesh,
        in_specs=(
            P(None, "gx", "gy", "gz"),
            P(("gx", "gy", "gz")),
            P(("gx", "gy", "gz"), None),
            P(("gx", "gy", "gz")),
            P(("gx", "gy", "gz")),
            P(None, ("gx", "gz")),
            P(("gx", "gz")),
        ),
        out_specs=(P(None, "gx", "gy", "gz"), P(None, "gx", "gy", "gz")),
        check_vma=False,
    )
```
